256 devices in a mesh: section: 2 (over core), dp: 8 (over z), head: 16 (over y, x).
Axes of the slice: x: 4, y: 4, z: 8, core: 2. Of those that a mesh axis runs over, the one named last changes fastest.
Arguments:
- tokens: bfloat16 [2048, 1600], P('dp'), may hold values from -6 to 6
- up_weight: bfloat16 [2, 1600, 6400], P('section', 'dp', 'head'), may hold values from -0.15625 to 0.15625
- down_weight: bfloat16 [2, 6400, 1600], P('section', 'head', 'dp'), may hold values from -0.078125 to 0.078125
- neck_weight: bfloat16 [1600, 1024], replicated, may hold values from -0.15625 to 0.15625
- casc_weight: bfloat16 [3, 1024, 1024], replicated, may hold values from -0.1875 to 0.1875
- class_weight: bfloat16 [3, 1024, 80], replicated, may hold values from -0.1875 to 0.1875
- roi_bins: int32 [4096, 16], P('dp'), may hold values from 0 to 255
- positive: int32 [4096], P('dp'), may hold values 0 or 1
- targets: int32 [4096, 3], P('dp'), may hold values from 0 to 79
Outputs:
- grad_up: float32 [2, 1600, 6400], P('section', 'dp', 'head')
- grad_down: float32 [2, 6400, 1600], P('section', 'head', 'dp')
The draws below stay inside these ranges and needn't reach their ends.
Inputs may be any that keep to these rules, and one draw needn't show every extreme that they name: `roi_bins`: the sample bins of a RoI index the 256 bins of its own image.
All inputs are finite; a program needn't handle non-finite values. No bound on the sum of `positive` on one device may be relied on, other than what follows from the above.
Results may differ from the reference program's by a relative error of at most 0.004.
Values may be sent and summed in bfloat16 or wider, within the bound.
A program may use at most 128 MiB of HBM per device.

```python
import jax
import jax.numpy as jnp
from jax import lax

D = 1600
FF = 6400
C = 1024
CLS = 80
CASC = 3
KSAMP = 16
ROIS = 512
LAYERS = 2
BINS = 256
TOKENS = 2048
ALLROIS = 4096
N_DP = 8


def plant(drawn, key, low, high):
    place = [jax.random.randint(jax.random.fold_in(key, axis), (), 0, length) for axis, length in enumerate(drawn.shape)]
    widest = drawn.shape.index(max(drawn.shape))
    neighbour = place[:widest] + [(place[widest] + 1) % drawn.shape[widest]] + place[widest + 1:]
    return drawn.at[tuple(place)].set(low).at[tuple(neighbour)].set(high)


def steps_of(key, extent, pieces, least, high):
    def one(position, blocks):
        heights = jax.random.uniform(jax.random.fold_in(jax.random.fold_in(key, 6), position), (blocks,), jnp.float32, least / len(pieces), high / len(pieces))
        return jnp.repeat(jnp.exp(heights), extent[position] // blocks).reshape((-1,) + (1,) * (len(extent) - position - 1))

    gain = one(*pieces[0])
    for cut in pieces[1:]:
        gain = gain * one(*cut)
    return gain


def normal_values(stream_key, dims, deviation, most, cuts=(), kind=jnp.bfloat16):
    gain = steps_of(stream_key, dims, cuts, -0.22, 0.18) if cuts else 1.0
    result = jax.random.normal(stream_key, dims, jnp.float32) * deviation * gain
    return jnp.minimum(jnp.maximum(result, -most), most).astype(kind)


def setup_inputs(seed: int = 0) -> dict:
    key_list = jax.random.split(jax.random.key(seed), 10)
    tokens = normal_values(key_list[0], (TOKENS, D), 1.0, 6.0, ((0, 8),))
    up_weight = normal_values(key_list[1], (LAYERS, D, FF), D ** -0.5, 0.15625, ((0, 2), (1, 8), (2, 16)))
    down_weight = normal_values(key_list[2], (LAYERS, FF, D), FF ** -0.5, 0.078125, ((0, 2), (1, 16), (2, 8)))
    neck_weight = normal_values(key_list[3], (D, C), D ** -0.5, 0.15625)
    casc_weight = normal_values(key_list[4], (CASC, C, C), C ** -0.5, 0.1875)
    class_weight = normal_values(key_list[5], (CASC, C, CLS), C ** -0.5, 0.1875)
    roi_bins = plant(jax.random.randint(key_list[6], (ALLROIS, KSAMP), 0, BINS), jax.random.fold_in(key_list[6], 1), 0, BINS - 1).astype(jnp.int32)
    positive = plant((jax.random.randint(key_list[7], (ALLROIS,), 0, 4) < 1).astype(jnp.int32), jax.random.fold_in(key_list[7], 1), 0, 1)
    targets = plant(jax.random.randint(key_list[8], (ALLROIS, CASC), 0, CLS), jax.random.fold_in(key_list[8], 1), 0, CLS - 1).astype(jnp.int32)
    return dict(tokens=tokens, up_weight=up_weight, down_weight=down_weight, neck_weight=neck_weight, casc_weight=casc_weight, class_weight=class_weight, roi_bins=roi_bins, positive=positive, targets=targets)


epsilon = 1e-06

def smooth_act(values):
    return jax.nn.gelu(values, approximate=True)

def smooth_slope(values):
    return jax.jvp(smooth_act, (values,), (jnp.ones_like(values),))[1]

def normalize(values):
    centre = values - lax.optimization_barrier(jnp.mean(values, axis=-1, keepdims=True))
    inv_std = lax.rsqrt(lax.optimization_barrier(jnp.mean(centre * centre, axis=-1, keepdims=True)) + epsilon)
    return (centre * inv_std, inv_std)

def norm_back(grad_in, scaled, inv_std):
    mean_one = lax.optimization_barrier(jnp.mean(grad_in, axis=-1, keepdims=True))
    mean_two = lax.optimization_barrier(jnp.mean(grad_in * scaled, axis=-1, keepdims=True))
    return inv_std * (grad_in - mean_one - scaled * mean_two)

def transpose_dot(left_side, right_side):
    return lax.dot_general(left_side, right_side, (((0,), (0,)), ((), ())), preferred_element_type=jnp.float32)

def dot_trans(left_side, right_side):
    return lax.dot_general(left_side, right_side, (((1,), (1,)), ((), ())), preferred_element_type=jnp.float32)

def pool_matrix(sample_bins, bins_total):
    matches = sample_bins[:, :, None] == jnp.arange(bins_total, dtype=jnp.int32)[None, None, :]
    counted = lax.optimization_barrier(jnp.sum(matches.astype(jnp.float32), axis=1))
    return (counted / sample_bins.shape[1]).astype(jnp.bfloat16)

def target_table(labels, positive, classes_total):
    matches = labels[:, :, None] == jnp.arange(classes_total, dtype=jnp.int32)[None, None, :]
    return matches.astype(jnp.float32) * positive[:, None, None].astype(jnp.float32)

def head_pass(pooled, casc_weight, class_weight, wanted):
    current = pooled
    inner_list = []
    outer_list = []
    for level_num in range(casc_weight.shape[0]):
        mixed_rows = jnp.dot(current, casc_weight[level_num], preferred_element_type=jnp.float32)
        inner_list.append(mixed_rows)
        current = (current.astype(jnp.float32) + smooth_act(mixed_rows)).astype(jnp.bfloat16)
        logits = jnp.dot(current, class_weight[level_num], preferred_element_type=jnp.float32)
        outer_list.append((jax.nn.sigmoid(logits) - wanted[:, level_num]).astype(jnp.bfloat16))
    running = jnp.zeros(pooled.shape, jnp.float32)
    for level_num in reversed(range(casc_weight.shape[0])):
        running = running + dot_trans(outer_list[level_num], class_weight[level_num])
        through = (running * smooth_slope(inner_list[level_num])).astype(jnp.bfloat16)
        running = running + dot_trans(through, casc_weight[level_num])
    return running.astype(jnp.bfloat16)

def image_pass(image_tokens, up_weight, down_weight, neck_weight, casc_weight, class_weight, sample_bins, positive, labels):
    saved_list = []
    current = image_tokens
    for layer_num in range(up_weight.shape[0]):
        scaled, inv_std = normalize(current.astype(jnp.float32))
        normed = scaled.astype(jnp.bfloat16)
        before = jnp.dot(normed, up_weight[layer_num], preferred_element_type=jnp.float32)
        active = smooth_act(before).astype(jnp.bfloat16)
        saved_list.append((current, normed, before, active))
        current = (current.astype(jnp.float32) + jnp.dot(active, down_weight[layer_num], preferred_element_type=jnp.float32)).astype(jnp.bfloat16)
    features = jnp.dot(current, neck_weight, preferred_element_type=jnp.float32).astype(jnp.bfloat16)
    pooling = pool_matrix(sample_bins, features.shape[0])
    pooled = jnp.dot(pooling, features, preferred_element_type=jnp.float32).astype(jnp.bfloat16)
    wanted = target_table(labels, positive, class_weight.shape[2])
    pooled_grad = head_pass(pooled, casc_weight, class_weight, wanted)
    feature_grad = transpose_dot(pooling, pooled_grad).astype(jnp.bfloat16)
    upstream = dot_trans(feature_grad, neck_weight).astype(jnp.bfloat16)
    grads_up = []
    grads_down = []
    for layer_num in reversed(range(up_weight.shape[0])):
        current, normed, before, active = saved_list[layer_num]
        hidden_grad = (dot_trans(upstream, down_weight[layer_num]) * smooth_slope(before)).astype(jnp.bfloat16)
        grads_down.insert(0, transpose_dot(active, upstream))
        grads_up.insert(0, transpose_dot(normed, hidden_grad))
        scaled, inv_std = normalize(current.astype(jnp.float32))
        normed_grad = dot_trans(hidden_grad, up_weight[layer_num])
        upstream = (upstream.astype(jnp.float32) + norm_back(normed_grad, scaled, inv_std)).astype(jnp.bfloat16)
    return (jnp.stack(grads_up), jnp.stack(grads_down))

def reference(tokens, up_weight, down_weight, neck_weight, casc_weight, class_weight, roi_bins, positive, targets):

    def one_image(totals, image_num):
        image_tokens = lax.dynamic_slice_in_dim(tokens, image_num * BINS, BINS, 0)
        sample_bins = lax.dynamic_slice_in_dim(roi_bins, image_num * ROIS, ROIS, 0)
        image_positive = lax.dynamic_slice_in_dim(positive, image_num * ROIS, ROIS, 0)
        image_targets = lax.dynamic_slice_in_dim(targets, image_num * ROIS, ROIS, 0)
        part_up, part_down = image_pass(image_tokens, up_weight, down_weight, neck_weight, casc_weight, class_weight, sample_bins, image_positive, image_targets)
        return ((totals[0] + part_up, totals[1] + part_down), None)
    start_totals = (jnp.zeros(up_weight.shape, jnp.float32), jnp.zeros(down_weight.shape, jnp.float32))
    totals, unused = lax.scan(one_image, start_totals, jnp.arange(N_DP, dtype=jnp.int32))
    return (totals[0], totals[1])
```

```python
import jax
import jax.numpy as jnp
from jax import lax
from jax.experimental import pallas as pl
from jax.experimental.pallas import tpu as pltpu
from jax.sharding import PartitionSpec as P

MESH = pl.DeviceIdType.MESH
EPS = 1e-06
BF = jnp.bfloat16
F32 = jnp.float32


def dot(a, b):
    return jnp.dot(a, b, preferred_element_type=F32)


def dot_rt(a, b):
    return lax.dot_general(a, b, (((1,), (1,)), ((), ())), preferred_element_type=F32)


def dot_lt(a, b):
    return lax.dot_general(a, b, (((0,), (0,)), ((), ())), preferred_element_type=F32)


def gelu_both(z):
    c = 0.7978845608028654
    zz = z * z
    t = jnp.tanh(c * z * (1.0 + 0.044715 * zz))
    half = 0.5 * (1.0 + t)
    slope = half + (0.5 * c) * z * (1.0 - t * t) * (1.0 + (3 * 0.044715) * zz)
    return z * half, slope


def norm_rows(x):
    centre = x - jnp.mean(x, axis=-1, keepdims=True)
    inv = lax.rsqrt(jnp.mean(centre * centre, axis=-1, keepdims=True) + EPS)
    return centre * inv, inv


def make_kernel(nd, nh, dims):
    rows, width, wsl, hid, chan, cls, levels, rois, ksamp = dims
    rb = rows // nh
    qb = rois // nh
    n_right = nd // 2
    n_left = nd - 1 - n_right

    def kernel(
        tokens, up, down, neck, casc, clsw, bins, labels, gup, gdn,
        upg, dng, xb, nrm, slope, act, hg, part, rs_a, rs_d, yall, ppart, prec, pg,
        xrow, nsb, nzr, nsl, ysb, ysb1, yzr, ysl, neckv, cascv, clsr, clsv, terms, binv, labv, poolv,
        lsem, ss, rs, zgo,
    ):
        s = lax.axis_index("section")
        d = lax.axis_index("dp")
        h = lax.axis_index("head")
        myrows = pl.ds(pl.multiple_of(h * rb, rb), rb)
        myrois = pl.ds(pl.multiple_of(h * qb, qb), qb)

        def loop(a, b, body):
            def step(k, c):
                body(k)
                return c

            lax.fori_loop(a, b, step, 0)

        def plane(row, src, dst, core):
            def make(k):
                t = lax.rem(h + k, nh)
                return pltpu.make_async_remote_copy(
                    src_ref=src(t), dst_ref=dst(k), send_sem=ss.at[row, k], recv_sem=rs.at[row, k],
                    device_id=(core, d, t), device_id_type=MESH,
                )

            return make

        def column(row, src, dst, core):
            def make(k):
                t = lax.rem(d + k, nd)
                return pltpu.make_async_remote_copy(
                    src_ref=src(t), dst_ref=dst(k), send_sem=ss.at[row, k], recv_sem=rs.at[row, k],
                    device_id=(core, t, h), device_id_type=MESH,
                )

            return make

        def ring(row, buf, relative, rights, lefts):
            def slot(j):
                return j if relative else lax.rem(d - j + nd, nd)

            def right(t):
                return pltpu.make_async_remote_copy(
                    src_ref=buf.at[slot(t)], dst_ref=buf.at[t + 1 if relative else slot(t)],
                    send_sem=ss.at[row, t + 1], recv_sem=rs.at[row, t + 1],
                    device_id=(s, lax.rem(d + 1, nd), h), device_id_type=MESH,
                )

            def left(t):
                j = (nd - t) % nd
                return pltpu.make_async_remote_copy(
                    src_ref=buf.at[slot(j)], dst_ref=buf.at[nd - 1 - t if relative else slot(j)],
                    send_sem=ss.at[row, nd - 1 - t], recv_sem=rs.at[row, nd - 1 - t],
                    device_id=(s, lax.rem(d + nd - 1, nd), h), device_id_type=MESH,
                )

            return [(right, rights), (left, lefts)]

        def ring_step(chains, t):
            for make, count in chains:
                if t < count:
                    if t > 0:
                        make(t - 1).wait_recv()
                    make(t).start()

        def ring_last(chains):
            for make, count in chains:
                make(count - 1).wait_recv()

        def ring_sent(chains):
            for make, count in chains:
                for t in range(count):
                    make(t).wait_send()

        load_up = pltpu.make_async_copy(up.at[0], upg.at[d], lsem.at[0])
        load_down = pltpu.make_async_copy(down.at[0], dng.at[d], lsem.at[1])
        load_up.start()
        load_down.start()
        barrier = pltpu.get_barrier_semaphore()

        def greet_plane(k):
            pl.semaphore_signal(barrier, inc=1, device_id=(s, d, lax.rem(h + k, nh)), device_id_type=MESH)

        def greet_plane_other(k):
            pl.semaphore_signal(barrier, inc=1, device_id=(1 - s, d, lax.rem(h + k, nh)), device_id_type=MESH)

        def greet_column(k):
            pl.semaphore_signal(barrier, inc=1, device_id=(s, lax.rem(d + k, nd), h), device_id_type=MESH)
            pl.semaphore_signal(barrier, inc=1, device_id=(1 - s, lax.rem(d + k, nd), h), device_id_type=MESH)

        loop(1, nd, greet_column)
        loop(1, nh, greet_plane)
        loop(0, nh, greet_plane_other)

        load_tok = pltpu.make_async_copy(tokens, xb, lsem.at[2])
        load_neck = pltpu.make_async_copy(neck, neckv, lsem.at[3])
        load_casc = pltpu.make_async_copy(casc, cascv, lsem.at[4])
        load_cls = pltpu.make_async_copy(clsw, clsr, lsem.at[5])
        load_bins = pltpu.make_async_copy(bins, binv, lsem.at[6])
        load_lab = pltpu.make_async_copy(labels, labv, lsem.at[7])
        load_tok.start()

        @pl.when(s == 1)
        def _():
            for c in (load_bins, load_lab, load_neck, load_casc, load_cls):
                c.start()

        load_up.wait()
        load_down.wait()
        pl.semaphore_wait(barrier, 2 * (nd - 1) + 2 * nh - 1)

        chains = ring(0, upg, False, n_right, n_left) + ring(1, dng, False, n_left, n_right)

        send_a = plane(2, lambda t: part.at[pl.ds(pl.multiple_of(t * rb, rb), rb)], lambda k: rs_a.at[k], 1)
        send_n = plane(3, lambda t: nrm.at[myrows], lambda k: nrm.at[myrows], 1)
        send_p = plane(4, lambda t: ppart.at[pl.ds(pl.multiple_of(t * qb, qb), qb)], lambda k: prec.at[k], 1)
        send_g = plane(5, lambda t: pg.at[myrois], lambda k: pg.at[myrois], 1)
        send_d = plane(6, lambda t: part.at[pl.ds(pl.multiple_of(t * rb, rb), rb)], lambda k: rs_d.at[k], 1)
        send_y = plane(7, lambda t: yall.at[myrows], lambda k: yall.at[myrows], 0)
        spread_n = plane(8, lambda t: nsl.at[:, myrows, :], lambda k: nsl.at[:, myrows, :], s)
        spread_y = plane(9, lambda t: ysl.at[:, myrows, :], lambda k: ysl.at[:, myrows, :], s)
        cross_n = column(10, lambda t: nsb.at[t], lambda k: nzr.at[k], s)
        cross_y2 = column(11, lambda t: ysb.at[t], lambda k: yzr.at[k], 1)
        cross_y1 = column(14, lambda t: ysb1.at[t], lambda k: yzr.at[k], 0)
        cross_act = column(12, lambda t: act.at[0], lambda k: act.at[k], s)
        cross_hg = column(13, lambda t: hg.at[0], lambda k: hg.at[k], 1)
        hg_ring = ring(13, hg, True, n_right, n_left)

        def start(make, a, b):
            loop(a, b, lambda k: make(k).start())

        def arrived(make, a, b):
            loop(a, b, lambda k: make(k).wait_recv())

        def sent(make, a, b):
            loop(a, b, lambda k: make(k).wait_send())

        def lanes(j):
            return slice(j * wsl, (j + 1) * wsl)

        def forward():
            before = dot(nrm[:, lanes(0)], upg[0])
            for j in range(1, nd):
                before = before + dot(nrm[:, lanes(j)], upg[j])
            value, rise = gelu_both(before)
            slope[...] = rise
            act[0] = value.astype(BF)

        def down_sum():
            active = act[0]
            for j in range(nd):
                part[:, lanes(j)] = dot(active, dng[j]).astype(BF)

        def backward():
            grad = dot_rt(yall[:, lanes(0)], dng[0])
            for j in range(1, nd):
                grad = grad + dot_rt(yall[:, lanes(j)], dng[j])
            hg[0] = (grad * slope[...]).astype(BF)

        def slots(dst, values):
            for j in range(nd):
                dst[j] = values[:, lanes(j)]

        def up_grad():
            total = dot_lt(nsl[0], hg[0])
            for j in range(1, nd):
                total = total + dot_lt(nsl[j], hg[j])
            gup[0] = total

        def down_grad():
            total = dot_lt(act[0], ysl[0])
            for j in range(1, nd):
                total = total + dot_lt(act[j], ysl[j])
            gdn[0] = total

        @pl.when(s == 0)
        def _():
            ring_step(chains, 0)
            load_tok.wait()
            nrm[...] = norm_rows(xb[...].astype(F32))[0].astype(BF)
            slots(nsb, nrm[myrows, :])
            for t in range(1, n_right):
                ring_step(chains, t)
            ring_last(chains)
            forward()
            down_sum()
            start(send_a, 0, nh)
            ring_sent(chains)
            pl.semaphore_signal(zgo, inc=1, device_id=(1, d, h), device_id_type=MESH)
            start(cross_n, 1, nd)
            pl.semaphore_wait(zgo, 1)
            start(cross_act, 1, nd)
            nsl[0, myrows, :] = nsb[d]
            arrived(cross_n, 1, nd)
            for j in range(1, nd):
                nsl[j, myrows, :] = nzr[j]
            sent(send_a, 0, nh)
            start(spread_n, 1, nh)
            arrived(cross_act, 1, nd)
            arrived(spread_n, 1, nh)
            sent(cross_n, 1, nd)
            sent(cross_act, 1, nd)
            sent(spread_n, 1, nh)
            arrived(send_y, 0, nh)
            backward()
            ring_step(hg_ring, 0)
            arrived(cross_y1, 0, nd)
            for j in range(nd):
                ysl[j, myrows, :] = yzr[j]
            start(spread_y, 1, nh)
            for t in range(1, n_right):
                ring_step(hg_ring, t)
            arrived(spread_y, 1, nh)
            down_grad()
            ring_last(hg_ring)
            up_grad()
            ring_sent(hg_ring)
            sent(spread_y, 1, nh)

        @pl.when(s == 1)
        def _():
            load_bins.wait()
            spots = lax.broadcasted_iota(jnp.int32, (rois, rows), 1)
            found = binv[...]
            count = jnp.zeros((rois, rows), F32)
            for j in range(ksamp):
                count = count + jnp.where(found[:, j : j + 1] == spots, 1.0, 0.0)
            poolv[...] = (count * (1.0 / ksamp)).astype(BF)
            load_tok.wait()
            load_lab.wait()
            load_neck.wait()
            load_casc.wait()
            load_cls.wait()
            clsv[...] = jnp.zeros(clsv.shape, BF)
            clsv[:, :, 0:cls] = clsr[...]
            pl.semaphore_wait(zgo, 1)
            for t in range(n_right):
                ring_step(chains, t)
            ring_last(chains)
            ring_sent(chains)
            pl.semaphore_signal(zgo, inc=1, device_id=(0, d, h), device_id_type=MESH)

            total = xb[myrows, :].astype(F32)
            arrived(send_a, 0, nh)
            for k in range(nh):
                total = total + rs_a[k].astype(F32)
            xrow[...] = total.astype(BF)
            normed = norm_rows(xrow[...].astype(F32))[0].astype(BF)
            nrm[myrows, :] = normed
            start(send_n, 1, nh)
            slots(nsb, normed)
            start(cross_n, 1, nd)
            arrived(send_n, 1, nh)
            forward()
            start(cross_act, 1, nd)
            down_sum()
            part[myrows, :] = (part[myrows, :].astype(F32) + xrow[...].astype(F32)).astype(BF)
            features = dot(part[...], neckv[...]).astype(BF)
            ppart[...] = dot(poolv[...], features).astype(BF)
            start(send_p, 1, nh)
            nsl[0, myrows, :] = nsb[d]
            arrived(cross_n, 1, nd)
            for j in range(1, nd):
                nsl[j, myrows, :] = nzr[j]
            total = ppart[myrois, :].astype(F32)
            arrived(send_p, 1, nh)
            start(spread_n, 1, nh)
            for k in range(1, nh):
                total = total + prec[k].astype(F32)

            current = total.astype(BF)
            wanted = labv[myrois, :]
            classes = lax.broadcasted_iota(jnp.int32, (qb, 128), 1)
            rises = []
            errors = []
            for j in range(levels):
                value, rise = gelu_both(dot(current, cascv[j]))
                rises.append(rise)
                current = (current.astype(F32) + value).astype(BF)
                logits = dot(current, clsv[j])
                hit = jnp.where(wanted[:, j : j + 1] == classes, 1.0, 0.0)
                errors.append(jnp.where(classes < cls, jax.nn.sigmoid(logits) - hit, 0.0).astype(BF))
                terms[2 * j] = dot_rt(errors[j], clsv[j])
            running = jnp.zeros((qb, chan), F32)
            for j in reversed(range(levels)):
                running = running + terms[2 * j]
                through = (running * rises[j]).astype(BF)
                terms[2 * j + 1] = dot_rt(through, cascv[j])
                running = running + terms[2 * j + 1]
            pg[myrois, :] = running.astype(BF)
            start(send_g, 1, nh)
            arrived(send_g, 1, nh)
            feature_grad = dot_lt(poolv[...], pg[...]).astype(BF)
            yall[...] = dot_rt(feature_grad, neckv[...]).astype(BF)

            backward()
            start(cross_hg, 1, nd)
            hidden = hg[0]
            for j in range(nd):
                part[:, lanes(j)] = dot_rt(hidden, upg[j]).astype(BF)
            start(send_d, 1, nh)
            slots(ysb, yall[myrows, :])
            start(cross_y2, 1, nd)
            scaled, inv = norm_rows(xrow[...].astype(F32))
            total = part[myrows, :].astype(F32)
            arrived(send_d, 1, nh)
            for k in range(1, nh):
                total = total + rs_d[k].astype(F32)
            mean_one = jnp.mean(total, axis=-1, keepdims=True)
            mean_two = jnp.mean(total * scaled, axis=-1, keepdims=True)
            y_one = (yall[myrows, :].astype(F32) + inv * (total - mean_one - scaled * mean_two)).astype(BF)
            yall[myrows, :] = y_one
            start(send_y, 0, nh)
            slots(ysb1, y_one)
            start(cross_y1, 0, nd)
            ysl[0, myrows, :] = ysb[d]
            arrived(cross_y2, 1, nd)
            for j in range(1, nd):
                ysl[j, myrows, :] = yzr[j]
            start(spread_y, 1, nh)
            arrived(spread_n, 1, nh)
            arrived(cross_hg, 1, nd)
            up_grad()
            arrived(cross_act, 1, nd)
            arrived(spread_y, 1, nh)
            down_grad()
            sent(send_n, 1, nh)
            sent(cross_n, 1, nd)
            sent(cross_act, 1, nd)
            sent(send_p, 1, nh)
            sent(spread_n, 1, nh)
            sent(send_g, 1, nh)
            sent(cross_hg, 1, nd)
            sent(send_d, 1, nh)
            sent(cross_y2, 1, nd)
            sent(send_y, 0, nh)
            sent(cross_y1, 0, nd)
            sent(spread_y, 1, nh)

    return kernel


def solution(mesh):
    nd, nh = mesh.shape["dp"], mesh.shape["head"]

    def per_device(tokens, up, down, neck, casc, clsw, bins, positive, targets):
        rows, width = tokens.shape
        wsl, hid = up.shape[1:]
        levels, chan, cls = clsw.shape
        rois, ksamp = bins.shape
        rb, qb = rows // nh, rois // nh
        labels = jnp.where(positive[:, None] == 1, targets, -1)
        vmem = pltpu.VMEM
        scratch = [
            vmem((nd, wsl, hid), BF), vmem((nd, hid, wsl), BF), vmem((rows, width), BF), vmem((rows, width), BF),
            vmem((rows, hid), F32), vmem((nd, rows, hid), BF), vmem((nd, rows, hid), BF), vmem((rows, width), BF),
            vmem((nh, rb, width), BF), vmem((nh, rb, width), BF), vmem((rows, width), BF),
            vmem((rois, chan), BF), vmem((nh, qb, chan), BF), vmem((rois, chan), BF),
            vmem((rb, width), BF), vmem((nd, rb, wsl), BF), vmem((nd, rb, wsl), BF), vmem((nd, rows, wsl), BF),
            vmem((nd, rb, wsl), BF), vmem((nd, rb, wsl), BF), vmem((nd, rb, wsl), BF), vmem((nd, rows, wsl), BF),
            vmem(neck.shape, BF), vmem(casc.shape, BF), vmem(clsw.shape, BF), vmem((levels, chan, 128), BF), vmem((2 * levels, qb, chan), F32),
            vmem(bins.shape, jnp.int32), vmem(labels.shape, jnp.int32), vmem((rois, rows), BF),
            pltpu.SemaphoreType.DMA((8,)), pltpu.SemaphoreType.DMA((15, 16)), pltpu.SemaphoreType.DMA((15, 16)),
            pltpu.SemaphoreType.REGULAR,
        ]
        kernel = make_kernel(nd, nh, (rows, width, wsl, hid, chan, cls, levels, rois, ksamp))
        return pl.pallas_call(
            kernel,
            out_shape=(
                jax.ShapeDtypeStruct((1, wsl, hid), F32),
                jax.ShapeDtypeStruct((1, hid, wsl), F32),
            ),
            in_specs=[pl.BlockSpec(memory_space=pl.ANY)] * 8,
            out_specs=[pl.BlockSpec(memory_space=vmem)] * 2,
            scratch_shapes=scratch,
            compiler_params=pltpu.CompilerParams(
                collective_id=1, has_side_effects=True, vmem_limit_bytes=56 * 2**20
            ),
            name="window",
        )(tokens, up, down, neck, casc, clsw, bins, labels)

    return jax.shard_map(
        per_device,
        mesh=mesh,
        in_specs=(
            P("dp", None), P("section", "dp", "head"), P("section", "head", "dp"), P(), P(), P(),
            P("dp", None), P("dp"), P("dp", None),
        ),
        out_specs=(P("section", "dp", "head"), P("section", "head", "dp")),
        check_vma=False,
    )
```

```python
import jax
import jax.numpy as jnp
from jax import lax
from jax.experimental import pallas as pl
from jax.experimental.pallas import tpu as pltpu
from jax.sharding import PartitionSpec as P

MESH = pl.DeviceIdType.MESH
EPS = 1e-06
BF = jnp.bfloat16
F32 = jnp.float32


def dot(a, b):
    return jnp.dot(a, b, preferred_element_type=F32)


def dot_rt(a, b):
    return lax.dot_general(a, b, (((1,), (1,)), ((), ())), preferred_element_type=F32)


def dot_lt(a, b):
    return lax.dot_general(a, b, (((0,), (0,)), ((), ())), preferred_element_type=F32)


def gelu_both(z):
    c = 0.7978845608028654
    zz = z * z
    t = jnp.tanh(c * z * (1.0 + 0.044715 * zz))
    half = 0.5 * (1.0 + t)
    slope = half + (0.5 * c) * z * (1.0 - t * t) * (1.0 + (3 * 0.044715) * zz)
    return z * half, slope


def norm_rows(x):
    centre = x - jnp.mean(x, axis=-1, keepdims=True)
    inv = lax.rsqrt(jnp.mean(centre * centre, axis=-1, keepdims=True) + EPS)
    return centre * inv, inv


def row_cuts(total, pieces):
    tiles = total // 16
    edges = [16 * (tiles * p // pieces) for p in range(pieces)] + [total]
    return [(a, b - a) for a, b in zip(edges, edges[1:])]


def hand_over(up_in, down_in, up_out, down_out):
    up_out[...] = up_in[...]
    down_out[...] = down_in[...]


def make_kernel(nd, nh, dims):
    rows, width, wsl, hid, chan, cls, levels, rois, ksamp = dims
    rb = rows // nh
    qb = rois // nh
    side = int(round(nh**0.5))
    n_right = nd // 2
    n_left = nd - 1 - n_right

    def kernel(
        tokens, up, down, neck, casc, clsw, bins, positive, targets, gup, gdn,
        upg, dng, xt, xb, nrm, slope, act, hg, part, rs_a, rs_d, yall, feat, ppart, prec, pg,
        xrow, yrow, nsb, nzr, nsl, ysb, ysb1, yzr, ysl, neckv, cascv, casct, clsr, clsv, clst, terms,
        binv, posv, tarv, hits, poolv, poolt, wv, wl, wt, wlt, lsem, ss, rs, ring_ss, ring_rs, zgo,
    ):
        s = lax.axis_index("section")
        d = lax.axis_index("dp")
        h = lax.axis_index("head")
        myrows = pl.ds(pl.multiple_of(h * rb, rb), rb)
        myrois = pl.ds(pl.multiple_of(h * qb, qb), qb)

        def loop(a, b, body):
            def step(k, c):
                body(k)
                return c

            lax.fori_loop(a, b, step, 0)

        far_plane = sorted(range(nh), key=lambda k: -sum(min(o, side - o) for o in (k // side, k % side)))
        far_column = sorted(range(nd), key=lambda k: -min(k, nd - k))

        def partner(k):
            return lax.rem(h // side + k // side, side) * side + lax.rem(h + k % side, side)

        def plane(row, src, dst, core):
            def make(k):
                t = partner(k)
                return pltpu.make_async_remote_copy(
                    src_ref=src(t), dst_ref=dst(k), send_sem=ss.at[row, k], recv_sem=rs.at[row, k],
                    device_id=(core, d, t), device_id_type=MESH,
                )

            return make

        def column(row, src, dst, core):
            def make(k):
                t = lax.rem(d + k, nd)
                return pltpu.make_async_remote_copy(
                    src_ref=src(t), dst_ref=dst(k), send_sem=ss.at[row, k], recv_sem=rs.at[row, k],
                    device_id=(core, t, h), device_id_type=MESH,
                )

            return make

        def ring(row, buf, relative, rights, lefts, cuts):
            def slot(j):
                return j if relative else lax.rem(d - j + nd, nd)

            def copy(src, dst, piece, to):
                return pltpu.make_async_remote_copy(
                    src_ref=buf.at[(slot(src), *cuts[piece])],
                    dst_ref=buf.at[(dst if relative else slot(src), *cuts[piece])],
                    send_sem=ring_ss.at[row, dst, piece], recv_sem=ring_rs.at[row, dst, piece],
                    device_id=(s, lax.rem(d + to, nd), h), device_id_type=MESH,
                )

            def right(t, piece):
                return copy(t, t + 1, piece, 1)

            def left(t, piece):
                return copy((nd - t) % nd, nd - 1 - t, piece, nd - 1)

            return [(right, rights, len(cuts)), (left, lefts, len(cuts))]

        def ring_step(chains, t):
            for piece in range(max(pieces for _, _, pieces in chains)):
                for make, count, pieces in chains:
                    if t < count and piece < pieces:
                        if t > 0:
                            make(t - 1, piece).wait_recv()
                        make(t, piece).start()

        def ring_last(chains):
            for make, count, pieces in chains:
                for piece in range(pieces):
                    make(count - 1, piece).wait_recv()

        def ring_sent(chains):
            for make, count, pieces in chains:
                for t in range(count):
                    for piece in range(pieces):
                        make(t, piece).wait_send()

        load_up = pltpu.make_async_copy(up.at[0], upg.at[d], lsem.at[0])
        load_down = pltpu.make_async_copy(down.at[0], dng.at[d], lsem.at[1])
        load_up.start()
        load_down.start()
        barrier = pltpu.get_barrier_semaphore()

        def greet_plane(k):
            pl.semaphore_signal(barrier, inc=1, device_id=(s, d, partner(k)), device_id_type=MESH)

        def greet_plane_other(k):
            pl.semaphore_signal(barrier, inc=1, device_id=(1 - s, d, partner(k)), device_id_type=MESH)

        def greet_column(k):
            pl.semaphore_signal(barrier, inc=1, device_id=(s, lax.rem(d + k, nd), h), device_id_type=MESH)
            pl.semaphore_signal(barrier, inc=1, device_id=(1 - s, lax.rem(d + k, nd), h), device_id_type=MESH)

        loop(1, nd, greet_column)
        loop(1, nh, greet_plane)
        loop(0, nh, greet_plane_other)

        load_tok = pltpu.make_async_copy(tokens, xt, lsem.at[2])
        load_neck = pltpu.make_async_copy(neck, neckv, lsem.at[3])
        load_casc = pltpu.make_async_copy(casc, cascv, lsem.at[4])
        load_cls = pltpu.make_async_copy(clsw, clsr, lsem.at[5])
        load_bins = pltpu.make_async_copy(bins, binv, lsem.at[6])
        load_pos = pltpu.make_async_copy(positive, posv, lsem.at[7])
        load_tar = pltpu.make_async_copy(targets, tarv, lsem.at[8])
        load_tok.start()

        @pl.when(s == 1)
        def _():
            for c in (load_bins, load_pos, load_tar, load_neck, load_casc, load_cls):
                c.start()

        load_up.wait()
        load_down.wait()
        pl.semaphore_wait(barrier, 2 * (nd - 1) + 2 * nh - 1)

        all_of = slice(None)
        up_cuts = [(all_of, slice(a, min(a + 128, hid))) for a in range(0, hid, 128)]
        down_cuts = [(pl.ds(a, n),) for a, n in row_cuts(hid, 4)]
        hg_cuts = [(pl.ds(a, n),) for a, n in row_cuts(rows, 4)]
        chains = ring(0, upg, False, n_right, n_left, up_cuts) + ring(1, dng, False, n_left, n_right, down_cuts)

        send_a = plane(2, lambda t: part.at[pl.ds(pl.multiple_of(t * rb, rb), rb)], lambda k: rs_a.at[k], 1)
        send_n = plane(3, lambda t: nrm.at[myrows], lambda k: nrm.at[myrows], 1)
        send_p = plane(4, lambda t: ppart.at[pl.ds(pl.multiple_of(t * qb, qb), qb)], lambda k: prec.at[k], 1)
        send_g = plane(5, lambda t: pg.at[myrois], lambda k: pg.at[myrois], 1)
        send_d = plane(6, lambda t: part.at[pl.ds(pl.multiple_of(t * rb, rb), rb)], lambda k: rs_d.at[k], 1)
        send_y = plane(7, lambda t: yall.at[myrows], lambda k: yall.at[myrows], 0)
        spread_n = plane(8, lambda t: nsl.at[:, myrows, :], lambda k: nsl.at[:, myrows, :], s)
        spread_y = plane(9, lambda t: ysl.at[:, myrows, :], lambda k: ysl.at[:, myrows, :], s)
        cross_n = column(10, lambda t: nsb.at[t], lambda k: nzr.at[k], s)
        cross_y2 = column(11, lambda t: ysb.at[t], lambda k: yzr.at[k], 1)
        cross_y1 = column(14, lambda t: ysb1.at[t], lambda k: yzr.at[k], 0)
        hg_ring = ring(2, hg, True, n_right, n_left, hg_cuts)
        act_ring = ring(3, act, True, n_left, n_right, hg_cuts)

        def start(make, a, b):
            order = far_plane if b == nh else far_column
            for k in order:
                if k >= a:
                    make(k).start()

        def arrived(make, a, b):
            loop(a, b, lambda k: make(k).wait_recv())

        def sent(make, a, b):
            loop(a, b, lambda k: make(k).wait_send())

        def lanes(j):
            return slice(j * wsl, (j + 1) * wsl)

        def forward():
            before = dot(nrm[:, lanes(0)], upg[0])
            for j in range(1, nd):
                before = before + dot(nrm[:, lanes(j)], upg[j])
            value, rise = gelu_both(before)
            slope[...] = rise
            act[0] = value.astype(BF)

        def down_sum():
            active = act[0]
            for j in range(nd):
                part[:, lanes(j)] = dot(active, dng[j]).astype(BF)

        def backward():
            grad = dot_rt(yall[:, lanes(0)], dng[0])
            for j in range(1, nd):
                grad = grad + dot_rt(yall[:, lanes(j)], dng[j])
            hg[0] = (grad * slope[...]).astype(BF)

        def slots(dst, values):
            for j in range(nd):
                dst[j] = values[:, lanes(j)]

        def up_grad(j):
            term = dot_lt(nsl[j], hg[j])
            gup[0] = term if j == 0 else gup[0] + term

        def down_grad():
            total = dot_lt(act[0], ysl[0])
            for j in range(1, nd):
                total = total + dot_lt(act[j], ysl[j])
            gdn[0] = total

        @pl.when(s == 0)
        def _():
            ring_step(chains, 0)
            load_tok.wait()
            xb[...] = xt[...].T
            nrm[...] = norm_rows(xb[...].astype(F32))[0].astype(BF)
            slots(nsb, nrm[myrows, :])
            for t in range(1, n_right):
                ring_step(chains, t)
            pl.semaphore_signal(zgo, inc=1, device_id=(1, d, h), device_id_type=MESH)
            ring_last(chains)
            forward()
            down_sum()
            start(send_a, 0, nh)
            start(cross_n, 1, nd)
            nsl[0, myrows, :] = nsb[d]
            pl.semaphore_wait(zgo, 1)
            ring_step(act_ring, 0)
            arrived(cross_n, 1, nd)
            for j in range(1, nd):
                nsl[j, myrows, :] = nzr[j]
            sent(send_a, 0, nh)
            for t in range(1, n_right):
                ring_step(act_ring, t)
            ring_last(act_ring)
            start(spread_n, 1, nh)
            arrived(spread_n, 1, nh)
            ring_sent(chains)
            ring_sent(act_ring)
            sent(cross_n, 1, nd)
            sent(spread_n, 1, nh)
            arrived(send_y, 0, nh)
            backward()
            ring_step(hg_ring, 0)
            arrived(cross_y1, 0, nd)
            for j in range(nd):
                ysl[j, myrows, :] = yzr[j]
            start(spread_y, 1, nh)
            up_grad(0)
            for t in range(1, n_right):
                ring_step(hg_ring, t)
                if t == 2:
                    arrived(spread_y, 1, nh)
                    down_grad()
                up_grad(t)
                if t < n_left:
                    up_grad(nd - t)
            ring_last(hg_ring)
            for t in range(n_right, nd - n_left + 1):
                up_grad(t)
            ring_sent(hg_ring)
            sent(spread_y, 1, nh)

        @pl.when(s == 1)
        def _():
            load_bins.wait()
            spots = lax.broadcasted_iota(jnp.int32, (rows, rois), 0)
            found = binv[...]
            count = jnp.zeros((rows, rois), F32)
            for j in range(ksamp):
                count = count + jnp.where(found[j : j + 1, :] == spots, 1.0, 0.0)
            poolt[...] = (count * (1.0 / ksamp)).astype(BF)
            poolv[...] = (count * (1.0 / ksamp)).T.astype(BF)
            load_pos.wait()
            load_tar.wait()
            classes = lax.broadcasted_iota(jnp.int32, (128, rois), 0)
            for j in range(levels):
                wanted = (tarv[j : j + 1, :] == classes) & (posv[...] == 1)
                hits[j] = jnp.where(wanted, 1.0, 0.0).T
            load_tok.wait()
            xb[...] = xt[...].T
            load_cls.wait()
            clsv[...] = jnp.zeros(clsv.shape, BF)
            clsv[:, 0:cls, :] = clsr[...]
            load_casc.wait()
            for j in range(levels):
                clst[j] = clsv[j].T
                casct[j] = cascv[j].T
            load_neck.wait()
            pl.semaphore_wait(zgo, 1)
            for t in range(n_right):
                ring_step(chains, t)
            ring_last(chains)
            pl.semaphore_signal(zgo, inc=1, device_id=(0, d, h), device_id_type=MESH)

            total = xb[myrows, :].astype(F32)
            arrived(send_a, 0, nh)
            for k in range(nh):
                total = total + rs_a[k].astype(F32)
            xrow[...] = total.astype(BF)
            normed = norm_rows(xrow[...].astype(F32))[0].astype(BF)
            nrm[myrows, :] = normed
            start(send_n, 1, nh)
            slots(nsb, normed)
            start(cross_n, 1, nd)
            both = dot(dng[0], neckv[0])
            kept = dot(xrow[:, lanes(0)], neckv[0])
            for j in range(1, nd):
                both = both + dot(dng[j], neckv[j])
                kept = kept + dot(xrow[:, lanes(j)], neckv[j])
            wv[...] = both.astype(BF)
            wl[...] = (both - wv[...].astype(F32)).astype(BF)
            arrived(send_n, 1, nh)
            forward()
            feat[...] = dot(act[0], wv[...]).astype(BF)
            feat[myrows, :] = (feat[myrows, :].astype(F32) + kept).astype(BF)
            ppart[...] = dot(poolv[...], feat[...]).astype(BF)
            start(send_p, 1, nh)
            ring_step(act_ring, 0)
            wt[...] = wv[...].T
            wlt[...] = wl[...].T
            nsl[0, myrows, :] = nsb[d]
            arrived(cross_n, 1, nd)
            for j in range(1, nd):
                nsl[j, myrows, :] = nzr[j]
            total = ppart[myrois, :].astype(F32)
            arrived(send_p, 1, nh)
            for k in range(1, nh):
                total = total + prec[k].astype(F32)

            ring_step(act_ring, 1)
            start(spread_n, 1, nh)

            current = total.astype(BF)
            lane = lax.broadcasted_iota(jnp.int32, (qb, 128), 1)
            rises = []
            for j in range(levels):
                value, rise = gelu_both(dot(current, cascv[j]))
                rises.append(rise)
                current = (current.astype(F32) + value).astype(BF)
                error = jax.nn.sigmoid(dot(current, clst[j])) - hits[j, myrois, :]
                error = jnp.where(lane < cls, error, 0.0).astype(BF)
                terms[2 * j] = dot(error, clsv[j])
            running = jnp.zeros((qb, chan), F32)
            for j in reversed(range(levels)):
                running = running + terms[2 * j]
                through = (running * rises[j]).astype(BF)
                terms[2 * j + 1] = dot(through, casct[j])
                running = running + terms[2 * j + 1]
            pg[myrois, :] = running.astype(BF)
            start(send_g, 1, nh)
            ring_step(act_ring, 2)
            ring_step(act_ring, 3)
            ring_last(act_ring)
            arrived(send_g, 1, nh)

            feat[...] = dot(poolt[...], pg[...]).astype(BF)
            grad = dot(feat[...], wt[...]) + dot(feat[...], wlt[...])
            hg[0] = (grad * slope[...]).astype(BF)
            ring_step(hg_ring, 0)
            hidden = hg[0]
            for j in range(nd):
                part[:, lanes(j)] = dot_rt(hidden, upg[j]).astype(BF)
            start(send_d, 1, nh)
            mine = feat[myrows, :]
            for j in range(nd):
                piece = dot_rt(mine, neckv[j]).astype(BF)
                ysb[j] = piece
                yrow[:, lanes(j)] = piece
            start(cross_y2, 1, nd)
            scaled, inv = norm_rows(xrow[...].astype(F32))
            total = part[myrows, :].astype(F32)
            ring_step(hg_ring, 1)
            arrived(send_d, 1, nh)
            for k in range(1, nh):
                total = total + rs_d[k].astype(F32)
            mean_one = jnp.mean(total, axis=-1, keepdims=True)
            mean_two = jnp.mean(total * scaled, axis=-1, keepdims=True)
            y_one = (yrow[...].astype(F32) + inv * (total - mean_one - scaled * mean_two)).astype(BF)
            yall[myrows, :] = y_one
            start(send_y, 0, nh)
            slots(ysb1, y_one)
            start(cross_y1, 0, nd)
            ring_step(hg_ring, 2)
            ysl[0, myrows, :] = ysb[d]
            arrived(cross_y2, 1, nd)
            for j in range(1, nd):
                ysl[j, myrows, :] = yzr[j]
            start(spread_y, 1, nh)
            arrived(spread_n, 1, nh)
            ring_step(hg_ring, 3)
            ring_last(hg_ring)
            for j in range(nd):
                up_grad(j)
            arrived(spread_y, 1, nh)
            down_grad()
            sent(send_n, 1, nh)
            sent(cross_n, 1, nd)
            ring_sent(act_ring)
            sent(send_p, 1, nh)
            sent(spread_n, 1, nh)
            sent(send_g, 1, nh)
            ring_sent(chains)
            ring_sent(hg_ring)
            sent(send_d, 1, nh)
            sent(cross_y2, 1, nd)
            sent(send_y, 0, nh)
            sent(cross_y1, 0, nd)
            sent(spread_y, 1, nh)

    return kernel


def solution(mesh):
    nd, nh = mesh.shape["dp"], mesh.shape["head"]

    def per_device(tokens, up, down, neck, casc, clsw, bins, positive, targets):
        rows, width = tokens.shape
        wsl, hid = up.shape[1:]
        levels, chan, cls = clsw.shape
        rois, ksamp = bins.shape
        rb, qb = rows // nh, rois // nh
        vmem = pltpu.VMEM
        scratch = [
            vmem((nd, wsl, hid), BF), vmem((nd, hid, wsl), BF), vmem((width, rows), BF),
            vmem((rows, width), BF), vmem((rows, width), BF),
            vmem((rows, hid), F32), vmem((nd, rows, hid), BF), vmem((nd, rows, hid), BF), vmem((rows, width), BF),
            vmem((nh, rb, width), BF), vmem((nh, rb, width), BF), vmem((rows, width), BF), vmem((rows, chan), BF),
            vmem((rois, chan), BF), vmem((nh, qb, chan), BF), vmem((rois, chan), BF),
            vmem((rb, width), BF), vmem((rb, width), BF),
            vmem((nd, rb, wsl), BF), vmem((nd, rb, wsl), BF), vmem((nd, rows, wsl), BF),
            vmem((nd, rb, wsl), BF), vmem((nd, rb, wsl), BF), vmem((nd, rb, wsl), BF), vmem((nd, rows, wsl), BF),
            vmem((nd, wsl, chan), BF), vmem(casc.shape, BF), vmem(casc.shape, BF),
            vmem((levels, cls, chan), BF), vmem((levels, 128, chan), BF), vmem((levels, chan, 128), BF),
            vmem((2 * levels, qb, chan), F32),
            vmem((ksamp, rois), jnp.int32), vmem((1, rois), jnp.int32), vmem((levels, rois), jnp.int32),
            vmem((levels, rois, 128), F32), vmem((rois, rows), BF), vmem((rows, rois), BF),
            vmem((hid, chan), BF), vmem((hid, chan), BF), vmem((chan, hid), BF), vmem((chan, hid), BF),
            pltpu.SemaphoreType.DMA((9,)), pltpu.SemaphoreType.DMA((15, 16)), pltpu.SemaphoreType.DMA((15, 16)),
            pltpu.SemaphoreType.DMA((4, nd, 4)), pltpu.SemaphoreType.DMA((4, nd, 4)),
            pltpu.SemaphoreType.REGULAR,
        ]
        kernel = make_kernel(nd, nh, (rows, width, wsl, hid, chan, cls, levels, rois, ksamp))
        results = pl.pallas_call(
            kernel,
            out_shape=(
                jax.ShapeDtypeStruct((1, wsl, hid), F32),
                jax.ShapeDtypeStruct((1, hid, wsl), F32),
            ),
            in_specs=[pl.BlockSpec(memory_space=pl.ANY)] * 9,
            out_specs=[pl.BlockSpec(memory_space=vmem)] * 2,
            scratch_shapes=scratch,
            compiler_params=pltpu.CompilerParams(
                collective_id=1, has_side_effects=True, vmem_limit_bytes=56 * 2**20
            ),
            name="window",
        )(
            tokens.T, up, down, neck.reshape(nd, wsl, chan), casc, clsw.transpose(0, 2, 1), bins.T,
            positive.reshape(1, rois), targets.T,
        )
        return pl.pallas_call(
            hand_over,
            out_shape=tuple(jax.ShapeDtypeStruct(r.shape, r.dtype) for r in results),
            in_specs=[pl.BlockSpec(memory_space=vmem)] * 2,
            out_specs=[pl.BlockSpec(memory_space=vmem)] * 2,
            name="hand_over",
        )(*results)

    return jax.shard_map(
        per_device,
        mesh=mesh,
        in_specs=(
            P("dp", None), P("section", "dp", "head"), P("section", "head", "dp"), P(), P(), P(),
            P("dp", None), P("dp"), P("dp", None),
        ),
        out_specs=(P("section", "dp", "head"), P("section", "head", "dp")),
        check_vma=False,
    )
```

```python
import jax
import jax.numpy as jnp
from jax import lax
from jax.experimental import pallas as pl
from jax.experimental.pallas import tpu as pltpu
from jax.sharding import PartitionSpec as P

MESH = pl.DeviceIdType.MESH
EPS = 1e-06
BF = jnp.bfloat16
F32 = jnp.float32


def dot(a, b):
    return jnp.dot(a, b, preferred_element_type=F32)


def dot_rt(a, b):
    return lax.dot_general(a, b, (((1,), (1,)), ((), ())), preferred_element_type=F32)


def dot_lt(a, b):
    return lax.dot_general(a, b, (((0,), (0,)), ((), ())), preferred_element_type=F32)


def gelu_both(z):
    c = 0.7978845608028654
    zz = z * z
    t = jnp.tanh(c * z * (1.0 + 0.044715 * zz))
    half = 0.5 * (1.0 + t)
    slope = half + (0.5 * c) * z * (1.0 - t * t) * (1.0 + (3 * 0.044715) * zz)
    return z * half, slope


def norm_rows(x):
    centre = x - jnp.mean(x, axis=-1, keepdims=True)
    inv = lax.rsqrt(jnp.mean(centre * centre, axis=-1, keepdims=True) + EPS)
    return centre * inv, inv


def row_cuts(total, pieces):
    tiles = total // 16
    edges = [16 * (tiles * p // pieces) for p in range(pieces)] + [total]
    return [(a, b - a) for a, b in zip(edges, edges[1:])]


def hand_over(up_in, down_in, up_out, down_out):
    up_out[...] = up_in[...]
    down_out[...] = down_in[...]


def make_kernel(nd, nh, dims):
    rows, width, wsl, hid, chan, cls, levels, rois, ksamp = dims
    rb = rows // nh
    qb = rois // nh
    side = int(round(nh**0.5))
    body = hid // 128 * 128
    rest = hid - body
    packed = rows + 16
    n_right = nd // 2
    n_left = nd - 1 - n_right

    def kernel(
        tokens, up, down, neck, casc, clsw, bins, positive, targets, gup, gdn,
        wg, dtg, upr, downr, xt, xb, nrm, slope, act, hg, last, part, rs_a, rs_d, yall, feat, ppart, prec, pg,
        xrow, yrow, nsb, nzr, nsl, ysb, ysb1, yzr, ysl, neckv, cascv, casct, clsr, clsv, clst, terms,
        binv, posv, tarv, hits, poolv, poolt, wv, wl, wt, wlt, lsem, ss, rs, ring_ss, ring_w, ring_h, ring_a, zgo,
    ):
        ring_rs = (ring_w, ring_h, ring_a)
        s = lax.axis_index("section")
        d = lax.axis_index("dp")
        h = lax.axis_index("head")
        myrows = pl.ds(pl.multiple_of(h * rb, rb), rb)
        myrois = pl.ds(pl.multiple_of(h * qb, qb), qb)

        def loop(a, b, body):
            def step(k, c):
                body(k)
                return c

            lax.fori_loop(a, b, step, 0)

        far_plane = sorted(range(nh), key=lambda k: -sum(min(o, side - o) for o in (k // side, k % side)))
        far_column = sorted(range(nd), key=lambda k: -min(k, nd - k))

        def partner(k):
            return lax.rem(h // side + k // side, side) * side + lax.rem(h + k % side, side)

        def exchange(row, src, dst, place, whole_src, whole_dst):
            def make(k):
                return pltpu.make_async_remote_copy(
                    src_ref=src(k), dst_ref=dst(k), send_sem=ss.at[row], recv_sem=rs.at[row],
                    device_id=place(k), device_id_type=MESH,
                )

            def whole():
                return pltpu.make_async_remote_copy(
                    src_ref=whole_src, dst_ref=whole_dst, send_sem=ss.at[row], recv_sem=rs.at[row],
                    device_id=place(1), device_id_type=MESH,
                )

            return make, whole

        def plane(row, src, dst, core, whole_src, whole_dst):
            def place(k):
                return (core, d, partner(k))

            return exchange(row, lambda k: src(partner(k)), dst, place, whole_src, whole_dst)

        def column(row, src, dst, core, whole_src, whole_dst):
            def place(k):
                return (core, lax.rem(d + k, nd), h)

            return exchange(row, lambda k: src(lax.rem(d + k, nd)), dst, place, whole_src, whole_dst)

        def ring(row, buf, relative, rights, lefts, cuts, whole):
            def slot(j):
                return j if relative else lax.rem(d - j + nd, nd)

            def copy(src, dst, piece, to):
                return pltpu.make_async_remote_copy(
                    src_ref=buf.at[(slot(src), *cuts[piece])],
                    dst_ref=buf.at[(dst if relative else slot(src), *cuts[piece])],
                    send_sem=ring_ss.at[row], recv_sem=ring_rs[row].at[dst - 1, piece],
                    device_id=(s, lax.rem(d + to, nd), h), device_id_type=MESH,
                )

            def right(t, piece):
                return copy(t, t + 1, piece, 1)

            def left(t, piece):
                return copy((nd - t) % nd, nd - 1 - t, piece, nd - 1)

            def all_sent():
                pltpu.make_async_remote_copy(
                    src_ref=whole, dst_ref=whole, send_sem=ring_ss.at[row], recv_sem=ring_rs[row].at[0, 0],
                    device_id=(s, lax.rem(d + 1, nd), h), device_id_type=MESH,
                ).wait_send()

            return [(right, rights, len(cuts), all_sent), (left, lefts, len(cuts), all_sent)]

        def ring_step(chains, t):
            for piece in range(max(c[2] for c in chains)):
                for make, count, pieces, _ in chains:
                    if t < count and piece < pieces:
                        if t > 0:
                            make(t - 1, piece).wait_recv()
                        make(t, piece).start()

        def ring_last(chains):
            for make, count, pieces, _ in chains:
                for piece in range(pieces):
                    make(count - 1, piece).wait_recv()

        def ring_sent(chains):
            chains[0][3]()

        load_up = pltpu.make_async_copy(up.at[0], upr, lsem.at[0])
        load_down = pltpu.make_async_copy(down.at[0], downr, lsem.at[1])
        load_up.start()
        load_down.start()
        barrier = pltpu.get_barrier_semaphore()

        def greet_plane(k):
            pl.semaphore_signal(barrier, inc=1, device_id=(s, d, partner(k)), device_id_type=MESH)

        def greet_plane_other(k):
            pl.semaphore_signal(barrier, inc=1, device_id=(1 - s, d, partner(k)), device_id_type=MESH)

        def greet_column(k):
            pl.semaphore_signal(barrier, inc=1, device_id=(s, lax.rem(d + k, nd), h), device_id_type=MESH)
            pl.semaphore_signal(barrier, inc=1, device_id=(1 - s, lax.rem(d + k, nd), h), device_id_type=MESH)

        loop(1, nd, greet_column)
        loop(1, nh, greet_plane)
        loop(0, nh, greet_plane_other)

        load_tok = pltpu.make_async_copy(tokens, xt, lsem.at[2])
        load_neck = pltpu.make_async_copy(neck, neckv, lsem.at[3])
        load_casc = pltpu.make_async_copy(casc, cascv, lsem.at[4])
        load_cls = pltpu.make_async_copy(clsw, clsr, lsem.at[5])
        load_bins = pltpu.make_async_copy(bins, binv, lsem.at[6])
        load_pos = pltpu.make_async_copy(positive, posv, lsem.at[7])
        load_tar = pltpu.make_async_copy(targets, tarv, lsem.at[8])
        load_tok.start()

        @pl.when(s == 1)
        def _():
            for c in (load_bins, load_pos, load_tar, load_neck, load_casc, load_cls):
                c.start()

        load_up.wait()
        wg[d, :, 0:hid] = upr[...]
        load_down.wait()
        wg[d, :, hid : 2 * hid] = downr[...].T
        pl.semaphore_wait(barrier, 2 * (nd - 1) + 2 * nh - 1)

        all_of = slice(None)
        mid = 4 * 128
        w_cuts = [(all_of, slice(0, 256)), (all_of, slice(256, mid)), (all_of, slice(mid, 2 * hid))]
        hg_cuts = [(pl.ds(a, n),) for a, n in row_cuts(packed, 4)]
        act_cuts = [(pl.ds(a, n),) for a, n in row_cuts(rows, 2)]
        chains = ring(0, wg, False, n_right, n_left, w_cuts, wg.at[pl.ds(0, nd - 1)])

        most = rows - rb
        others = pl.ds(0, most)
        send_a = plane(0, lambda t: part.at[pl.ds(pl.multiple_of(t * rb, rb), rb)], lambda k: rs_a.at[k], 1, part, rs_a)
        send_n = plane(1, lambda t: nrm.at[myrows], lambda k: nrm.at[myrows], 1, nrm.at[others], nrm.at[others])
        send_p = plane(
            2, lambda t: ppart.at[pl.ds(pl.multiple_of(t * qb, qb), qb)], lambda k: prec.at[k], 1,
            ppart.at[pl.ds(0, rois - qb)], prec.at[pl.ds(0, nh - 1)],
        )
        send_g = plane(
            3, lambda t: pg.at[myrois], lambda k: pg.at[myrois], 1,
            pg.at[pl.ds(0, rois - qb)], pg.at[pl.ds(0, rois - qb)],
        )
        send_d = plane(
            4, lambda t: part.at[pl.ds(pl.multiple_of(t * rb, rb), rb)], lambda k: rs_d.at[k], 1,
            part.at[others], rs_d.at[pl.ds(0, nh - 1)],
        )
        send_y = plane(5, lambda t: yall.at[myrows], lambda k: yall.at[myrows], 0, yall, yall)
        spread_n = plane(
            6, lambda t: nsl.at[:, myrows, :], lambda k: nsl.at[:, myrows, :], s,
            nsl.at[:, others, :], nsl.at[:, others, :],
        )
        spread_y = plane(
            7, lambda t: ysl.at[:, myrows, :], lambda k: ysl.at[:, myrows, :], s,
            ysl.at[:, others, :], ysl.at[:, others, :],
        )
        few = pl.ds(0, nd - 1)
        cross_n = column(8, lambda t: nsb.at[t], lambda k: nzr.at[k], s, nsb.at[few], nzr.at[few])
        cross_y2 = column(9, lambda t: ysb.at[t], lambda k: yzr.at[k], 1, ysb.at[few], yzr.at[few])
        cross_y1 = column(10, lambda t: ysb1.at[t], lambda k: yzr.at[k], 0, ysb1, yzr)
        hg_ring = ring(1, hg, True, n_right, n_left, hg_cuts, hg.at[few])
        act_ring = ring(2, act, True, n_left, n_right, act_cuts, act.at[few])

        def start(transfer, a, b):
            order = far_plane if b == nh else far_column
            for k in order:
                if k >= a:
                    transfer[0](k).start()

        def arrived(transfer):
            transfer[1]().wait_recv()

        def sent(transfer):
            transfer[1]().wait_send()

        def lanes(j):
            return slice(j * wsl, (j + 1) * wsl)

        def forward():
            before = dot(nrm[:, lanes(0)], wg[0, :, 0:hid])
            for j in range(1, nd):
                before = before + dot(nrm[:, lanes(j)], wg[j, :, 0:hid])
            value, rise = gelu_both(before)
            slope[...] = rise
            act[0] = value.astype(BF)

        def down_sum():
            active = act[0]
            for j in range(nd):
                part[:, lanes(j)] = dot_rt(active, dtg[j]).astype(BF)

        def keep_hidden(values):
            hg[0, 0:rows, :] = values[:, 0:body]
            for r in range(rows // 16):
                hg[0, rows:packed, r * rest : (r + 1) * rest] = values[16 * r : 16 * r + 16, body:hid]

        def backward():
            grad = dot(yall[:, lanes(0)], dtg[0])
            for j in range(1, nd):
                grad = grad + dot(yall[:, lanes(j)], dtg[j])
            keep_hidden((grad * slope[...]).astype(BF))

        def slots(dst, values):
            for j in range(nd):
                dst[j] = values[:, lanes(j)]

        def up_grad(j):
            for r in range(rows // 16):
                last[16 * r : 16 * r + 16, :] = hg[j, rows:packed, r * rest : (r + 1) * rest]
            term = dot_lt(nsl[j], hg[j, 0:rows, :])
            end = dot_lt(nsl[j], last[...])
            gup[0, :, 0:body] = term if j == 0 else gup[0, :, 0:body] + term
            gup[0, :, body:hid] = end if j == 0 else gup[0, :, body:hid] + end

        def down_grad():
            total = dot_lt(act[0], ysl[0])
            for j in range(1, nd):
                total = total + dot_lt(act[j], ysl[j])
            gdn[0] = total

        @pl.when(s == 0)
        def _():
            ring_step(chains, 0)
            load_tok.wait()
            xb[...] = xt[...].T
            nrm[...] = norm_rows(xb[...].astype(F32))[0].astype(BF)
            slots(nsb, nrm[myrows, :])
            for t in range(1, n_right):
                ring_step(chains, t)
                if t == 2:
                    pl.semaphore_signal(zgo, inc=1, device_id=(1, d, h), device_id_type=MESH)
            ring_last(chains)
            for j in range(nd):
                dtg[j] = wg[j, :, hid : 2 * hid]
            forward()
            down_sum()
            start(send_a, 0, nh)
            start(cross_n, 1, nd)
            nsl[0, myrows, :] = nsb[d]
            pl.semaphore_wait(zgo, 1)
            ring_step(act_ring, 0)
            arrived(cross_n)
            for j in range(1, nd):
                nsl[j, myrows, :] = nzr[j]
            sent(send_a)
            for t in range(1, n_right):
                ring_step(act_ring, t)
            ring_last(act_ring)
            start(spread_n, 1, nh)
            arrived(spread_n)
            ring_sent(chains)
            ring_sent(act_ring)
            sent(cross_n)
            sent(spread_n)
            arrived(send_y)
            backward()
            ring_step(hg_ring, 0)
            arrived(cross_y1)
            for j in range(nd):
                ysl[j, myrows, :] = yzr[j]
            start(spread_y, 1, nh)
            up_grad(0)
            for t in range(1, n_right):
                ring_step(hg_ring, t)
                if t == 2:
                    arrived(spread_y)
                    down_grad()
                up_grad(t)
                if t < n_left:
                    up_grad(nd - t)
            ring_last(hg_ring)
            for t in range(n_right, nd - n_left + 1):
                up_grad(t)
            ring_sent(hg_ring)
            sent(spread_y)

        @pl.when(s == 1)
        def _():
            load_bins.wait()
            spots = lax.broadcasted_iota(jnp.int32, (rows, rois), 0)
            found = binv[...]
            count = jnp.zeros((rows, rois), F32)
            for j in range(ksamp):
                count = count + jnp.where(found[j : j + 1, :] == spots, 1.0, 0.0)
            poolt[...] = (count * (1.0 / ksamp)).astype(BF)
            poolv[...] = (count * (1.0 / ksamp)).T.astype(BF)
            load_pos.wait()
            load_tar.wait()
            classes = lax.broadcasted_iota(jnp.int32, (128, rois), 0)
            for j in range(levels):
                wanted = (tarv[j : j + 1, :] == classes) & (posv[...] == 1)
                hits[j] = jnp.where(wanted, 1.0, 0.0).T
            load_tok.wait()
            xb[...] = xt[...].T
            load_cls.wait()
            clsv[...] = jnp.zeros(clsv.shape, BF)
            clsv[:, 0:cls, :] = clsr[...]
            load_casc.wait()
            for j in range(levels):
                clst[j] = clsv[j].T
                casct[j] = cascv[j].T
            load_neck.wait()
            pl.semaphore_wait(zgo, 1)
            for t in range(n_right):
                ring_step(chains, t)
            ring_last(chains)
            for j in range(nd):
                dtg[j] = wg[j, :, hid : 2 * hid]
            pl.semaphore_signal(zgo, inc=1, device_id=(0, d, h), device_id_type=MESH)

            total = xb[myrows, :].astype(F32)
            arrived(send_a)
            for k in range(nh):
                total = total + rs_a[k].astype(F32)
            xrow[...] = total.astype(BF)
            normed = norm_rows(xrow[...].astype(F32))[0].astype(BF)
            nrm[myrows, :] = normed
            start(send_n, 1, nh)
            slots(nsb, normed)
            start(cross_n, 1, nd)
            both = dot_lt(dtg[0], neckv[0])
            kept = dot(xrow[:, lanes(0)], neckv[0])
            for j in range(1, nd):
                both = both + dot_lt(dtg[j], neckv[j])
                kept = kept + dot(xrow[:, lanes(j)], neckv[j])
            wv[...] = both.astype(BF)
            wl[...] = (both - wv[...].astype(F32)).astype(BF)
            arrived(send_n)
            forward()
            feat[...] = dot(act[0], wv[...]).astype(BF)
            feat[myrows, :] = (feat[myrows, :].astype(F32) + kept).astype(BF)
            ppart[...] = dot(poolv[...], feat[...]).astype(BF)
            start(send_p, 1, nh)
            ring_step(act_ring, 0)
            wt[...] = wv[...].T
            wlt[...] = wl[...].T
            nsl[0, myrows, :] = nsb[d]
            arrived(cross_n)
            for j in range(1, nd):
                nsl[j, myrows, :] = nzr[j]
            total = ppart[myrois, :].astype(F32)
            arrived(send_p)
            for k in range(1, nh):
                total = total + prec[k].astype(F32)

            ring_step(act_ring, 1)
            start(spread_n, 1, nh)

            current = total.astype(BF)
            lane = lax.broadcasted_iota(jnp.int32, (qb, 128), 1)
            rises = []
            for j in range(levels):
                value, rise = gelu_both(dot(current, cascv[j]))
                rises.append(rise)
                current = (current.astype(F32) + value).astype(BF)
                error = jax.nn.sigmoid(dot(current, clst[j])) - hits[j, myrois, :]
                error = jnp.where(lane < cls, error, 0.0).astype(BF)
                terms[2 * j] = dot(error, clsv[j])
            running = jnp.zeros((qb, chan), F32)
            for j in reversed(range(levels)):
                running = running + terms[2 * j]
                through = (running * rises[j]).astype(BF)
                terms[2 * j + 1] = dot(through, casct[j])
                running = running + terms[2 * j + 1]
            pg[myrois, :] = running.astype(BF)
            start(send_g, 1, nh)
            ring_step(act_ring, 2)
            ring_step(act_ring, 3)
            ring_last(act_ring)
            arrived(send_g)

            feat[...] = dot(poolt[...], pg[...]).astype(BF)
            grad = dot(feat[...], wt[...]) + dot(feat[...], wlt[...])
            hidden = (grad * slope[...]).astype(BF)
            keep_hidden(hidden)
            ring_step(hg_ring, 0)
            for j in range(nd):
                part[:, lanes(j)] = dot_rt(hidden, wg[j, :, 0:hid]).astype(BF)
            start(send_d, 1, nh)
            mine = feat[myrows, :]
            for j in range(nd):
                piece = dot_rt(mine, neckv[j]).astype(BF)
                ysb[j] = piece
                yrow[:, lanes(j)] = piece
            start(cross_y2, 1, nd)
            scaled, inv = norm_rows(xrow[...].astype(F32))
            total = part[myrows, :].astype(F32)
            ring_step(hg_ring, 1)
            arrived(send_d)
            for k in range(1, nh):
                total = total + rs_d[k].astype(F32)
            mean_one = jnp.mean(total, axis=-1, keepdims=True)
            mean_two = jnp.mean(total * scaled, axis=-1, keepdims=True)
            y_one = (yrow[...].astype(F32) + inv * (total - mean_one - scaled * mean_two)).astype(BF)
            yall[myrows, :] = y_one
            start(send_y, 0, nh)
            slots(ysb1, y_one)
            start(cross_y1, 0, nd)
            ring_step(hg_ring, 2)
            ysl[0, myrows, :] = ysb[d]
            arrived(cross_y2)
            for j in range(1, nd):
                ysl[j, myrows, :] = yzr[j]
            start(spread_y, 1, nh)
            arrived(spread_n)
            ring_step(hg_ring, 3)
            ring_last(hg_ring)
            for j in range(nd):
                up_grad(j)
            arrived(spread_y)
            down_grad()
            sent(send_n)
            sent(cross_n)
            ring_sent(act_ring)
            sent(send_p)
            sent(spread_n)
            sent(send_g)
            ring_sent(chains)
            ring_sent(hg_ring)
            sent(send_d)
            sent(cross_y2)
            sent(send_y)
            sent(cross_y1)
            sent(spread_y)

    return kernel


def solution(mesh):
    nd, nh = mesh.shape["dp"], mesh.shape["head"]

    def per_device(tokens, up, down, neck, casc, clsw, bins, positive, targets):
        rows, width = tokens.shape
        wsl, hid = up.shape[1:]
        levels, chan, cls = clsw.shape
        rois, ksamp = bins.shape
        rb, qb = rows // nh, rois // nh
        vmem = pltpu.VMEM
        scratch = [
            vmem((nd, wsl, 2 * hid), BF), vmem((nd, wsl, hid), BF), vmem((wsl, hid), BF), vmem((hid, wsl), BF),
            vmem((width, rows), BF),
            vmem((rows, width), BF), vmem((rows, width), BF),
            vmem((rows, hid), F32), vmem((nd, rows, hid), BF), vmem((nd, rows + 16, hid // 128 * 128), BF),
            vmem((rows, hid % 128), BF), vmem((rows, width), BF),
            vmem((nh, rb, width), BF), vmem((nh, rb, width), BF), vmem((rows, width), BF), vmem((rows, chan), BF),
            vmem((rois, chan), BF), vmem((nh, qb, chan), BF), vmem((rois, chan), BF),
            vmem((rb, width), BF), vmem((rb, width), BF),
            vmem((nd, rb, wsl), BF), vmem((nd, rb, wsl), BF), vmem((nd, rows, wsl), BF),
            vmem((nd, rb, wsl), BF), vmem((nd, rb, wsl), BF), vmem((nd, rb, wsl), BF), vmem((nd, rows, wsl), BF),
            vmem((nd, wsl, chan), BF), vmem(casc.shape, BF), vmem(casc.shape, BF),
            vmem((levels, cls, chan), BF), vmem((levels, 128, chan), BF), vmem((levels, chan, 128), BF),
            vmem((2 * levels, qb, chan), F32),
            vmem((ksamp, rois), jnp.int32), vmem((1, rois), jnp.int32), vmem((levels, rois), jnp.int32),
            vmem((levels, rois, 128), F32), vmem((rois, rows), BF), vmem((rows, rois), BF),
            vmem((hid, chan), BF), vmem((hid, chan), BF), vmem((chan, hid), BF), vmem((chan, hid), BF),
            pltpu.SemaphoreType.DMA((9,)), pltpu.SemaphoreType.DMA((11,)), pltpu.SemaphoreType.DMA((11,)),
            pltpu.SemaphoreType.DMA((3,)), pltpu.SemaphoreType.DMA((nd - 1, 3)), pltpu.SemaphoreType.DMA((nd - 1, 4)),
            pltpu.SemaphoreType.DMA((nd - 1, 2)),
            pltpu.SemaphoreType.REGULAR,
        ]
        kernel = make_kernel(nd, nh, (rows, width, wsl, hid, chan, cls, levels, rois, ksamp))
        results = pl.pallas_call(
            kernel,
            out_shape=(
                jax.ShapeDtypeStruct((1, wsl, hid), F32),
                jax.ShapeDtypeStruct((1, hid, wsl), F32),
            ),
            in_specs=[pl.BlockSpec(memory_space=pl.ANY)] * 9,
            out_specs=[pl.BlockSpec(memory_space=vmem)] * 2,
            scratch_shapes=scratch,
            compiler_params=pltpu.CompilerParams(
                collective_id=1, has_side_effects=True, vmem_limit_bytes=56 * 2**20
            ),
            name="window",
        )(
            tokens.T, up, down, neck.reshape(nd, wsl, chan), casc, clsw.transpose(0, 2, 1), bins.T,
            positive.reshape(1, rois), targets.T,
        )
        return pl.pallas_call(
            hand_over,
            out_shape=tuple(jax.ShapeDtypeStruct(r.shape, r.dtype) for r in results),
            in_specs=[pl.BlockSpec(memory_space=vmem)] * 2,
            out_specs=[pl.BlockSpec(memory_space=vmem)] * 2,
            name="hand_over",
        )(*results)

    return jax.shard_map(
        per_device,
        mesh=mesh,
        in_specs=(
            P("dp", None), P("section", "dp", "head"), P("section", "head", "dp"), P(), P(), P(),
            P("dp", None), P("dp"), P("dp", None),
        ),
        out_specs=(P("section", "dp", "head"), P("section", "head", "dp")),
        check_vma=False,
    )
```

```python
import jax
import jax.numpy as jnp
from jax import lax
from jax.experimental import pallas as pl
from jax.experimental.pallas import tpu as pltpu
from jax.sharding import PartitionSpec as P

MESH = pl.DeviceIdType.MESH
EPS = 1e-06
BF = jnp.bfloat16
F32 = jnp.float32


def dot(a, b):
    return jnp.dot(a, b, preferred_element_type=F32)


def dot_rt(a, b):
    return lax.dot_general(a, b, (((1,), (1,)), ((), ())), preferred_element_type=F32)


def dot_lt(a, b):
    return lax.dot_general(a, b, (((0,), (0,)), ((), ())), preferred_element_type=F32)


def gelu_both(z):
    c = 0.7978845608028654
    zz = z * z
    t = jnp.tanh(c * z * (1.0 + 0.044715 * zz))
    half = 0.5 * (1.0 + t)
    slope = half + (0.5 * c) * z * (1.0 - t * t) * (1.0 + (3 * 0.044715) * zz)
    return z * half, slope


def norm_rows(x):
    centre = x - jnp.mean(x, axis=-1, keepdims=True)
    inv = lax.rsqrt(jnp.mean(centre * centre, axis=-1, keepdims=True) + EPS)
    return centre * inv, inv


def row_cuts(total, pieces):
    tiles = total // 16
    edges = [16 * (tiles * p // pieces) for p in range(pieces)] + [total]
    return [(a, b - a) for a, b in zip(edges, edges[1:])]


def hand_over(up_in, down_in, up_out, down_out):
    up_out[...] = up_in[...]
    down_out[...] = down_in[...]


def make_kernel(nd, nh, dims):
    rows, width, wsl, hid, chan, cls, levels, rois, ksamp = dims
    rb = rows // nh
    qb = rois // nh
    side = int(round(nh**0.5))
    body = hid // 128 * 128
    rest = hid - body
    packed = rows + 16
    n_right = nd // 2
    n_left = nd - 1 - n_right

    def kernel(
        tokens, up, down, neck, casc, clsw, bins, positive, targets, gup, gdn,
        wg, dtg, upr, downr, xt, xb, nrm, slope, act, act_b, hg, last, part, rs_a, rs_d, yall, feat, ppart, prec, pg,
        xrow, yrow, nsb, nzr, nsl, ysb, ysb1, yzr, ysl, neckv, cascv, casct, clsr, clsv, clst, terms,
        binv, posv, tarv, hits, poolv, poolt, wv, wl, wt, wlt, lsem, ss, rs, ring_ss, ring_w, ring_h, ring_a, ring_b, zgo,
    ):
        ring_rs = (ring_w, ring_h, ring_a, ring_b)
        s = lax.axis_index("section")
        d = lax.axis_index("dp")
        h = lax.axis_index("head")
        myrows = pl.ds(pl.multiple_of(h * rb, rb), rb)
        myrois = pl.ds(pl.multiple_of(h * qb, qb), qb)

        def loop(a, b, body):
            def step(k, c):
                body(k)
                return c

            lax.fori_loop(a, b, step, 0)

        far_plane = sorted(range(nh), key=lambda k: -sum(min(o, side - o) for o in (k // side, k % side)))
        far_column = sorted(range(nd), key=lambda k: -min(k, nd - k))

        def partner(k):
            return lax.rem(h // side + k // side, side) * side + lax.rem(h + k % side, side)

        def exchange(row, src, dst, place, whole_src, whole_dst):
            def make(k):
                return pltpu.make_async_remote_copy(
                    src_ref=src(k), dst_ref=dst(k), send_sem=ss.at[row], recv_sem=rs.at[row],
                    device_id=place(k), device_id_type=MESH,
                )

            def whole():
                return pltpu.make_async_remote_copy(
                    src_ref=whole_src, dst_ref=whole_dst, send_sem=ss.at[row], recv_sem=rs.at[row],
                    device_id=place(1), device_id_type=MESH,
                )

            return make, whole

        def plane(row, src, dst, core, whole_src, whole_dst):
            def place(k):
                return (core, d, partner(k))

            return exchange(row, lambda k: src(partner(k)), dst, place, whole_src, whole_dst)

        def column(row, src, dst, core, whole_src, whole_dst):
            def place(k):
                return (core, lax.rem(d + k, nd), h)

            return exchange(row, lambda k: src(lax.rem(d + k, nd)), dst, place, whole_src, whole_dst)

        def ring(row, buf, relative, rights, lefts, cuts, whole):
            def slot(j):
                return j if relative else lax.rem(d - j + nd, nd)

            def copy(src, dst, piece, to):
                return pltpu.make_async_remote_copy(
                    src_ref=buf.at[(slot(src), *cuts[piece])],
                    dst_ref=buf.at[(dst if relative else slot(src), *cuts[piece])],
                    send_sem=ring_ss.at[row], recv_sem=ring_rs[row].at[dst - 1, piece],
                    device_id=(s, lax.rem(d + to, nd), h), device_id_type=MESH,
                )

            def right(t, piece):
                return copy(t, t + 1, piece, 1)

            def left(t, piece):
                return copy((nd - t) % nd, nd - 1 - t, piece, nd - 1)

            def all_sent():
                pltpu.make_async_remote_copy(
                    src_ref=whole, dst_ref=whole, send_sem=ring_ss.at[row], recv_sem=ring_rs[row].at[0, 0],
                    device_id=(s, lax.rem(d + 1, nd), h), device_id_type=MESH,
                ).wait_send()

            return [(right, rights, len(cuts), all_sent), (left, lefts, len(cuts), all_sent)]

        def ring_step(chains, t):
            for piece in range(max(c[2] for c in chains)):
                for make, count, pieces, _ in chains:
                    if t < count and piece < pieces:
                        if t > 0:
                            make(t - 1, piece).wait_recv()
                        make(t, piece).start()

        def ring_last(chains):
            for make, count, pieces, _ in chains:
                for piece in range(pieces):
                    make(count - 1, piece).wait_recv()

        def ring_sent(chains):
            chains[0][3]()

        load_up = pltpu.make_async_copy(up.at[0], upr, lsem.at[0])
        load_down = pltpu.make_async_copy(down.at[0], downr, lsem.at[1])
        load_up.start()
        load_down.start()
        barrier = pltpu.get_barrier_semaphore()

        def greet_plane(k):
            pl.semaphore_signal(barrier, inc=1, device_id=(s, d, partner(k)), device_id_type=MESH)

        def greet_plane_other(k):
            pl.semaphore_signal(barrier, inc=1, device_id=(1 - s, d, partner(k)), device_id_type=MESH)

        def greet_column(k):
            pl.semaphore_signal(barrier, inc=1, device_id=(s, lax.rem(d + k, nd), h), device_id_type=MESH)
            pl.semaphore_signal(barrier, inc=1, device_id=(1 - s, lax.rem(d + k, nd), h), device_id_type=MESH)

        loop(1, nd, greet_column)
        loop(1, nh, greet_plane)
        loop(0, nh, greet_plane_other)

        load_tok = pltpu.make_async_copy(tokens, xt, lsem.at[2])
        load_neck = pltpu.make_async_copy(neck, neckv, lsem.at[3])
        load_casc = pltpu.make_async_copy(casc, cascv, lsem.at[4])
        load_cls = pltpu.make_async_copy(clsw, clsr, lsem.at[5])
        load_bins = pltpu.make_async_copy(bins, binv, lsem.at[6])
        load_pos = pltpu.make_async_copy(positive, posv, lsem.at[7])
        load_tar = pltpu.make_async_copy(targets, tarv, lsem.at[8])
        load_tok.start()

        @pl.when(s == 1)
        def _():
            for c in (load_bins, load_pos, load_tar, load_neck, load_casc, load_cls):
                c.start()

        load_up.wait()
        wg[d, :, 0:hid] = upr[...]
        load_down.wait()
        wg[d, :, hid : 2 * hid] = downr[...].T
        pl.semaphore_wait(barrier, 2 * (nd - 1) + 2 * nh - 1)

        all_of = slice(None)
        mid = 4 * 128
        w_cuts = [(all_of, slice(0, 256)), (all_of, slice(256, mid)), (all_of, slice(mid, 2 * hid))]
        hg_cuts = [(pl.ds(a, n),) for a, n in row_cuts(packed, 4)]
        act_cuts = [(pl.ds(a, n),) for a, n in row_cuts(rows, 2)]
        chains = ring(0, wg, False, n_right, n_left, w_cuts, wg.at[pl.ds(0, nd - 1)])

        most = rows - rb
        others = pl.ds(0, most)
        send_a = plane(0, lambda t: part.at[pl.ds(pl.multiple_of(t * rb, rb), rb)], lambda k: rs_a.at[k], 1, part, rs_a)
        send_n = plane(1, lambda t: nrm.at[myrows], lambda k: nrm.at[myrows], 1, nrm.at[others], nrm.at[others])
        send_p = plane(
            2, lambda t: ppart.at[pl.ds(pl.multiple_of(t * qb, qb), qb)], lambda k: prec.at[k], 1,
            ppart.at[pl.ds(0, rois - qb)], prec.at[pl.ds(0, nh - 1)],
        )
        send_g = plane(
            3, lambda t: pg.at[myrois], lambda k: pg.at[myrois], 1,
            pg.at[pl.ds(0, rois - qb)], pg.at[pl.ds(0, rois - qb)],
        )
        send_d = plane(
            4, lambda t: part.at[pl.ds(pl.multiple_of(t * rb, rb), rb)], lambda k: rs_d.at[k], 1,
            part.at[others], rs_d.at[pl.ds(0, nh - 1)],
        )
        send_y = plane(5, lambda t: yall.at[myrows], lambda k: yall.at[myrows], 0, yall, yall)
        spread_n = plane(
            6, lambda t: nsl.at[:, myrows, :], lambda k: nsl.at[:, myrows, :], s,
            nsl.at[:, others, :], nsl.at[:, others, :],
        )
        spread_y = plane(
            7, lambda t: ysl.at[:, myrows, :], lambda k: ysl.at[:, myrows, :], s,
            ysl.at[:, others, :], ysl.at[:, others, :],
        )
        few = pl.ds(0, nd - 1)
        cross_n = column(8, lambda t: nsb.at[t], lambda k: nzr.at[k], s, nsb.at[few], nzr.at[few])
        cross_y2 = column(9, lambda t: ysb.at[t], lambda k: yzr.at[k], 1, ysb.at[few], yzr.at[few])
        cross_y1 = column(10, lambda t: ysb1.at[t], lambda k: yzr.at[k], 0, ysb1, yzr)
        hg_ring = ring(1, hg, True, n_right, n_left, hg_cuts, hg.at[few])
        act_b_ring = ring(3, act_b, True, n_right, n_left, act_cuts, act_b.at[few])
        rounds = pl.ds(1, nd - 1)
        lend = pltpu.make_async_remote_copy(
            src_ref=act.at[0], dst_ref=act_b.at[0], send_sem=ss.at[11], recv_sem=rs.at[11],
            device_id=(1 - s, d, h), device_id_type=MESH,
        )
        give_back = pltpu.make_async_remote_copy(
            src_ref=act_b.at[rounds], dst_ref=act.at[rounds], send_sem=ss.at[12], recv_sem=rs.at[12],
            device_id=(1 - s, d, h), device_id_type=MESH,
        )
        act_ring = ring(2, act, True, n_left, n_right, act_cuts, act.at[few])

        def start(transfer, a, b):
            order = far_plane if b == nh else far_column
            for k in order:
                if k >= a:
                    transfer[0](k).start()

        def arrived(transfer):
            transfer[1]().wait_recv()

        def sent(transfer):
            transfer[1]().wait_send()

        def lanes(j):
            return slice(j * wsl, (j + 1) * wsl)

        def forward():
            before = dot(nrm[:, lanes(0)], wg[0, :, 0:hid])
            for j in range(1, nd):
                before = before + dot(nrm[:, lanes(j)], wg[j, :, 0:hid])
            value, rise = gelu_both(before)
            slope[...] = rise
            act[0] = value.astype(BF)

        def down_sum():
            active = act[0]
            for j in range(nd):
                part[:, lanes(j)] = dot_rt(active, dtg[j]).astype(BF)

        def keep_hidden(values):
            hg[0, 0:rows, :] = values[:, 0:body]
            for r in range(rows // 16):
                hg[0, rows:packed, r * rest : (r + 1) * rest] = values[16 * r : 16 * r + 16, body:hid]

        def backward():
            grad = dot(yall[:, lanes(0)], dtg[0])
            for j in range(1, nd):
                grad = grad + dot(yall[:, lanes(j)], dtg[j])
            keep_hidden((grad * slope[...]).astype(BF))

        def slots(dst, values):
            for j in range(nd):
                dst[j] = values[:, lanes(j)]

        def up_grad(j):
            for r in range(rows // 16):
                last[16 * r : 16 * r + 16, :] = hg[j, rows:packed, r * rest : (r + 1) * rest]
            term = dot_lt(nsl[j], hg[j, 0:rows, :])
            end = dot_lt(nsl[j], last[...])
            gup[0, :, 0:body] = term if j == 0 else gup[0, :, 0:body] + term
            gup[0, :, body:hid] = end if j == 0 else gup[0, :, body:hid] + end

        def down_grad():
            total = dot_lt(act[0], ysl[0])
            for j in range(1, nd):
                total = total + dot_lt(act[j], ysl[j])
            gdn[0] = total

        @pl.when(s == 0)
        def _():
            ring_step(chains, 0)
            load_tok.wait()
            xb[...] = xt[...].T
            nrm[...] = norm_rows(xb[...].astype(F32))[0].astype(BF)
            slots(nsb, nrm[myrows, :])
            nsl[0, myrows, :] = nsb[d]
            start(cross_n, 1, nd)
            for t in range(1, n_right):
                ring_step(chains, t)
                if t == 1:
                    arrived(cross_n)
                    for j in range(1, nd):
                        nsl[j, myrows, :] = nzr[j]
                    start(spread_n, 1, nh)
                if t == 2:
                    pl.semaphore_signal(zgo, inc=1, device_id=(1, d, h), device_id_type=MESH)
            ring_last(chains)
            for j in range(nd):
                dtg[j] = wg[j, :, hid : 2 * hid]
            forward()
            down_sum()
            start(send_a, 0, nh)
            pl.semaphore_wait(zgo, 1)
            for t in range(n_right):
                ring_step(act_ring, t)
            ring_last(act_ring)
            lend.wait_recv()
            for t in range(n_right):
                ring_step(act_b_ring, t)
            ring_last(act_b_ring)
            give_back.start()
            arrived(spread_n)
            sent(send_a)
            ring_sent(chains)
            ring_sent(act_ring)
            ring_sent(act_b_ring)
            sent(cross_n)
            sent(spread_n)
            arrived(send_y)
            backward()
            ring_step(hg_ring, 0)
            arrived(cross_y1)
            for j in range(nd):
                ysl[j, myrows, :] = yzr[j]
            start(spread_y, 1, nh)
            up_grad(0)
            for t in range(1, n_right):
                ring_step(hg_ring, t)
                if t == 2:
                    arrived(spread_y)
                    down_grad()
                up_grad(t)
                if t < n_left:
                    up_grad(nd - t)
            ring_last(hg_ring)
            for t in range(n_right, nd - n_left + 1):
                up_grad(t)
            give_back.wait_send()
            ring_sent(hg_ring)
            sent(spread_y)

        @pl.when(s == 1)
        def _():
            load_bins.wait()
            spots = lax.broadcasted_iota(jnp.int32, (rows, rois), 0)
            found = binv[...]
            count = jnp.zeros((rows, rois), F32)
            for j in range(ksamp):
                count = count + jnp.where(found[j : j + 1, :] == spots, 1.0, 0.0)
            poolt[...] = (count * (1.0 / ksamp)).astype(BF)
            poolv[...] = (count * (1.0 / ksamp)).T.astype(BF)
            load_pos.wait()
            load_tar.wait()
            classes = lax.broadcasted_iota(jnp.int32, (128, rois), 0)
            for j in range(levels):
                wanted = (tarv[j : j + 1, :] == classes) & (posv[...] == 1)
                hits[j] = jnp.where(wanted, 1.0, 0.0).T
            load_tok.wait()
            xb[...] = xt[...].T
            load_cls.wait()
            clsv[...] = jnp.zeros(clsv.shape, BF)
            clsv[:, 0:cls, :] = clsr[...]
            load_casc.wait()
            for j in range(levels):
                clst[j] = clsv[j].T
                casct[j] = cascv[j].T
            load_neck.wait()
            pl.semaphore_wait(zgo, 1)
            for t in range(n_right):
                ring_step(chains, t)
            ring_last(chains)
            for j in range(nd):
                dtg[j] = wg[j, :, hid : 2 * hid]
            pl.semaphore_signal(zgo, inc=1, device_id=(0, d, h), device_id_type=MESH)

            total = xb[myrows, :].astype(F32)
            arrived(send_a)
            for k in range(nh):
                total = total + rs_a[k].astype(F32)
            xrow[...] = total.astype(BF)
            normed = norm_rows(xrow[...].astype(F32))[0].astype(BF)
            nrm[myrows, :] = normed
            start(send_n, 1, nh)
            slots(nsb, normed)
            start(cross_n, 1, nd)
            both = dot_lt(dtg[0], neckv[0])
            kept = dot(xrow[:, lanes(0)], neckv[0])
            for j in range(1, nd):
                both = both + dot_lt(dtg[j], neckv[j])
                kept = kept + dot(xrow[:, lanes(j)], neckv[j])
            wv[...] = both.astype(BF)
            wl[...] = (both - wv[...].astype(F32)).astype(BF)
            arrived(send_n)
            forward()
            feat[...] = dot(act[0], wv[...]).astype(BF)
            feat[myrows, :] = (feat[myrows, :].astype(F32) + kept).astype(BF)
            ppart[...] = dot(poolv[...], feat[...]).astype(BF)
            start(send_p, 1, nh)
            lend.start()
            wt[...] = wv[...].T
            wlt[...] = wl[...].T
            nsl[0, myrows, :] = nsb[d]
            arrived(cross_n)
            for j in range(1, nd):
                nsl[j, myrows, :] = nzr[j]
            total = ppart[myrois, :].astype(F32)
            arrived(send_p)
            for k in range(1, nh):
                total = total + prec[k].astype(F32)

            start(spread_n, 1, nh)

            current = total.astype(BF)
            lane = lax.broadcasted_iota(jnp.int32, (qb, 128), 1)
            rises = []
            for j in range(levels):
                value, rise = gelu_both(dot(current, cascv[j]))
                rises.append(rise)
                current = (current.astype(F32) + value).astype(BF)
                error = jax.nn.sigmoid(dot(current, clst[j])) - hits[j, myrois, :]
                error = jnp.where(lane < cls, error, 0.0).astype(BF)
                terms[2 * j] = dot(error, clsv[j])
            running = jnp.zeros((qb, chan), F32)
            for j in reversed(range(levels)):
                running = running + terms[2 * j]
                through = (running * rises[j]).astype(BF)
                terms[2 * j + 1] = dot(through, casct[j])
                running = running + terms[2 * j + 1]
            pg[myrois, :] = running.astype(BF)
            start(send_g, 1, nh)
            arrived(send_g)

            feat[...] = dot(poolt[...], pg[...]).astype(BF)
            grad = dot(feat[...], wt[...]) + dot(feat[...], wlt[...])
            hidden = (grad * slope[...]).astype(BF)
            keep_hidden(hidden)
            ring_step(hg_ring, 0)
            for j in range(nd):
                part[:, lanes(j)] = dot_rt(hidden, wg[j, :, 0:hid]).astype(BF)
            start(send_d, 1, nh)
            mine = feat[myrows, :]
            for j in range(nd):
                piece = dot_rt(mine, neckv[j]).astype(BF)
                ysb[j] = piece
                yrow[:, lanes(j)] = piece
            start(cross_y2, 1, nd)
            scaled, inv = norm_rows(xrow[...].astype(F32))
            total = part[myrows, :].astype(F32)
            ring_step(hg_ring, 1)
            arrived(send_d)
            for k in range(1, nh):
                total = total + rs_d[k].astype(F32)
            mean_one = jnp.mean(total, axis=-1, keepdims=True)
            mean_two = jnp.mean(total * scaled, axis=-1, keepdims=True)
            y_one = (yrow[...].astype(F32) + inv * (total - mean_one - scaled * mean_two)).astype(BF)
            yall[myrows, :] = y_one
            start(send_y, 0, nh)
            slots(ysb1, y_one)
            start(cross_y1, 0, nd)
            ring_step(hg_ring, 2)
            ysl[0, myrows, :] = ysb[d]
            arrived(cross_y2)
            for j in range(1, nd):
                ysl[j, myrows, :] = yzr[j]
            start(spread_y, 1, nh)
            arrived(spread_n)
            ring_step(hg_ring, 3)
            ring_last(hg_ring)
            for j in range(nd):
                up_grad(j)
            give_back.wait_recv()
            arrived(spread_y)
            down_grad()
            sent(send_n)
            sent(cross_n)
            lend.wait_send()
            sent(send_p)
            sent(spread_n)
            sent(send_g)
            ring_sent(chains)
            ring_sent(hg_ring)
            sent(send_d)
            sent(cross_y2)
            sent(send_y)
            sent(cross_y1)
            sent(spread_y)

    return kernel


def solution(mesh):
    nd, nh = mesh.shape["dp"], mesh.shape["head"]

    def per_device(tokens, up, down, neck, casc, clsw, bins, positive, targets):
        rows, width = tokens.shape
        wsl, hid = up.shape[1:]
        levels, chan, cls = clsw.shape
        rois, ksamp = bins.shape
        rb, qb = rows // nh, rois // nh
        vmem = pltpu.VMEM
        scratch = [
            vmem((nd, wsl, 2 * hid), BF), vmem((nd, wsl, hid), BF), vmem((wsl, hid), BF), vmem((hid, wsl), BF),
            vmem((width, rows), BF),
            vmem((rows, width), BF), vmem((rows, width), BF),
            vmem((rows, hid), F32), vmem((nd, rows, hid), BF), vmem((nd, rows, hid), BF),
            vmem((nd, rows + 16, hid // 128 * 128), BF),
            vmem((rows, hid % 128), BF), vmem((rows, width), BF),
            vmem((nh, rb, width), BF), vmem((nh, rb, width), BF), vmem((rows, width), BF), vmem((rows, chan), BF),
            vmem((rois, chan), BF), vmem((nh, qb, chan), BF), vmem((rois, chan), BF),
            vmem((rb, width), BF), vmem((rb, width), BF),
            vmem((nd, rb, wsl), BF), vmem((nd, rb, wsl), BF), vmem((nd, rows, wsl), BF),
            vmem((nd, rb, wsl), BF), vmem((nd, rb, wsl), BF), vmem((nd, rb, wsl), BF), vmem((nd, rows, wsl), BF),
            vmem((nd, wsl, chan), BF), vmem(casc.shape, BF), vmem(casc.shape, BF),
            vmem((levels, cls, chan), BF), vmem((levels, 128, chan), BF), vmem((levels, chan, 128), BF),
            vmem((2 * levels, qb, chan), F32),
            vmem((ksamp, rois), jnp.int32), vmem((1, rois), jnp.int32), vmem((levels, rois), jnp.int32),
            vmem((levels, rois, 128), F32), vmem((rois, rows), BF), vmem((rows, rois), BF),
            vmem((hid, chan), BF), vmem((hid, chan), BF), vmem((chan, hid), BF), vmem((chan, hid), BF),
            pltpu.SemaphoreType.DMA((9,)), pltpu.SemaphoreType.DMA((13,)), pltpu.SemaphoreType.DMA((13,)),
            pltpu.SemaphoreType.DMA((4,)), pltpu.SemaphoreType.DMA((nd - 1, 3)), pltpu.SemaphoreType.DMA((nd - 1, 4)),
            pltpu.SemaphoreType.DMA((nd - 1, 2)), pltpu.SemaphoreType.DMA((nd - 1, 2)),
            pltpu.SemaphoreType.REGULAR,
        ]
        kernel = make_kernel(nd, nh, (rows, width, wsl, hid, chan, cls, levels, rois, ksamp))
        results = pl.pallas_call(
            kernel,
            out_shape=(
                jax.ShapeDtypeStruct((1, wsl, hid), F32),
                jax.ShapeDtypeStruct((1, hid, wsl), F32),
            ),
            in_specs=[pl.BlockSpec(memory_space=pl.ANY)] * 9,
            out_specs=[pl.BlockSpec(memory_space=vmem)] * 2,
            scratch_shapes=scratch,
            compiler_params=pltpu.CompilerParams(
                collective_id=1, has_side_effects=True, vmem_limit_bytes=56 * 2**20
            ),
            name="window",
        )(
            tokens.T, up, down, neck.reshape(nd, wsl, chan), casc, clsw.transpose(0, 2, 1), bins.T,
            positive.reshape(1, rois), targets.T,
        )
        return pl.pallas_call(
            hand_over,
            out_shape=tuple(jax.ShapeDtypeStruct(r.shape, r.dtype) for r in results),
            in_specs=[pl.BlockSpec(memory_space=vmem)] * 2,
            out_specs=[pl.BlockSpec(memory_space=vmem)] * 2,
            name="hand_over",
        )(*results)

    return jax.shard_map(
        per_device,
        mesh=mesh,
        in_specs=(
            P("dp", None), P("section", "dp", "head"), P("section", "head", "dp"), P(), P(), P(),
            P("dp", None), P("dp"), P("dp", None),
        ),
        out_specs=(P("section", "dp", "head"), P("section", "head", "dp")),
        check_vma=False,
    )
```

```python
import jax
import jax.numpy as jnp
from jax import lax
from jax.experimental import pallas as pl
from jax.experimental.pallas import tpu as pltpu
from jax.sharding import PartitionSpec as P

MESH = pl.DeviceIdType.MESH
EPS = 1e-06
BF = jnp.bfloat16
F32 = jnp.float32


def dot(a, b):
    return jnp.dot(a, b, preferred_element_type=F32)


def dot_rt(a, b):
    return lax.dot_general(a, b, (((1,), (1,)), ((), ())), preferred_element_type=F32)


def dot_lt(a, b):
    return lax.dot_general(a, b, (((0,), (0,)), ((), ())), preferred_element_type=F32)


def gelu_both(z):
    c = 0.7978845608028654
    zz = z * z
    t = jnp.tanh(c * z * (1.0 + 0.044715 * zz))
    half = 0.5 * (1.0 + t)
    slope = half + (0.5 * c) * z * (1.0 - t * t) * (1.0 + (3 * 0.044715) * zz)
    return z * half, slope


def norm_rows(x):
    centre = x - jnp.mean(x, axis=-1, keepdims=True)
    inv = lax.rsqrt(jnp.mean(centre * centre, axis=-1, keepdims=True) + EPS)
    return centre * inv, inv


def row_cuts(total, pieces):
    tiles = total // 16
    edges = [16 * (tiles * p // pieces) for p in range(pieces)] + [total]
    return [(a, b - a) for a, b in zip(edges, edges[1:])]


def hand_over(up_in, down_in, up_out, down_out):
    up_out[...] = up_in[...]
    down_out[...] = down_in[...]


def make_kernel(nd, nh, dims):
    rows, width, wsl, hid, chan, cls, levels, rois, ksamp = dims
    rb = rows // nh
    qb = rois // nh
    side = int(round(nh**0.5))
    body = hid // 128 * 128
    rest = hid - body
    packed = rows + 16
    n_right = nd // 2
    n_left = nd - 1 - n_right

    def kernel(
        tokens, up, down, neck, casc, clsw, bins, positive, targets, gup, gdn,
        wg, dtg, upr, downr, xt, xb, nrm, slope, act, act_b, hg, last, part, rs_a, rs_d, yall, feat, ppart, prec, pg,
        xrow, yrow, nsb, nzr, nsl, ysb, ysb1, yzr, ysl, neckv, cascv, casct, clsr, clsv, clst, terms,
        binv, posv, tarv, hits, poolv, poolt, wv, wl, wt, wlt, lsem, ss, rs, ring_ss, ring_w, ring_h, ring_a, ring_b, zgo,
    ):
        ring_rs = (ring_w, ring_h, ring_a, ring_b)
        s = lax.axis_index("section")
        d = lax.axis_index("dp")
        h = lax.axis_index("head")
        myrows = pl.ds(pl.multiple_of(h * rb, rb), rb)
        myrois = pl.ds(pl.multiple_of(h * qb, qb), qb)

        def loop(a, b, body):
            def step(k, c):
                body(k)
                return c

            lax.fori_loop(a, b, step, 0)

        far_plane = sorted(range(nh), key=lambda k: -sum(min(o, side - o) for o in (k // side, k % side)))
        far_column = sorted(range(nd), key=lambda k: -min(k, nd - k))

        def partner(k):
            return lax.rem(h // side + k // side, side) * side + lax.rem(h + k % side, side)

        def exchange(row, src, dst, place, whole_src, whole_dst):
            def make(k):
                return pltpu.make_async_remote_copy(
                    src_ref=src(k), dst_ref=dst(k), send_sem=ss.at[row], recv_sem=rs.at[row],
                    device_id=place(k), device_id_type=MESH,
                )

            def whole():
                return pltpu.make_async_remote_copy(
                    src_ref=whole_src, dst_ref=whole_dst, send_sem=ss.at[row], recv_sem=rs.at[row],
                    device_id=place(1), device_id_type=MESH,
                )

            return make, whole

        def plane(row, src, dst, core, whole_src, whole_dst):
            def place(k):
                return (core, d, partner(k))

            return exchange(row, lambda k: src(partner(k)), dst, place, whole_src, whole_dst)

        def column(row, src, dst, core, whole_src, whole_dst):
            def place(k):
                return (core, lax.rem(d + k, nd), h)

            return exchange(row, lambda k: src(lax.rem(d + k, nd)), dst, place, whole_src, whole_dst)

        def ring(row, buf, relative, rights, lefts, cuts, whole):
            def slot(j):
                return j if relative else lax.rem(d - j + nd, nd)

            def copy(src, dst, piece, to):
                return pltpu.make_async_remote_copy(
                    src_ref=buf.at[(slot(src), *cuts[piece])],
                    dst_ref=buf.at[(dst if relative else slot(src), *cuts[piece])],
                    send_sem=ring_ss.at[row], recv_sem=ring_rs[row].at[dst - 1, piece],
                    device_id=(s, lax.rem(d + to, nd), h), device_id_type=MESH,
                )

            def right(t, piece):
                return copy(t, t + 1, piece, 1)

            def left(t, piece):
                return copy((nd - t) % nd, nd - 1 - t, piece, nd - 1)

            def all_sent():
                pltpu.make_async_remote_copy(
                    src_ref=whole, dst_ref=whole, send_sem=ring_ss.at[row], recv_sem=ring_rs[row].at[0, 0],
                    device_id=(s, lax.rem(d + 1, nd), h), device_id_type=MESH,
                ).wait_send()

            return [(right, rights, len(cuts), all_sent), (left, lefts, len(cuts), all_sent)]

        def ring_step(chains, t):
            for piece in range(max(c[2] for c in chains)):
                for make, count, pieces, _ in chains:
                    if t < count and piece < pieces:
                        if t > 0:
                            make(t - 1, piece).wait_recv()
                        make(t, piece).start()

        def ring_last(chains):
            for make, count, pieces, _ in chains:
                for piece in range(pieces):
                    make(count - 1, piece).wait_recv()

        def ring_sent(chains):
            chains[0][3]()

        load_up = pltpu.make_async_copy(up.at[0], upr, lsem.at[0])
        load_down = pltpu.make_async_copy(down.at[0], downr, lsem.at[1])
        load_up.start()
        load_down.start()
        barrier = pltpu.get_barrier_semaphore()

        def greet_plane(k):
            pl.semaphore_signal(barrier, inc=1, device_id=(s, d, partner(k)), device_id_type=MESH)

        def greet_plane_other(k):
            pl.semaphore_signal(barrier, inc=1, device_id=(1 - s, d, partner(k)), device_id_type=MESH)

        def greet_column(k):
            pl.semaphore_signal(barrier, inc=1, device_id=(s, lax.rem(d + k, nd), h), device_id_type=MESH)
            pl.semaphore_signal(barrier, inc=1, device_id=(1 - s, lax.rem(d + k, nd), h), device_id_type=MESH)

        loop(1, nd, greet_column)
        loop(1, nh, greet_plane)
        loop(0, nh, greet_plane_other)

        load_tok = pltpu.make_async_copy(tokens, xt, lsem.at[2])
        load_neck = pltpu.make_async_copy(neck, neckv, lsem.at[3])
        load_casc = pltpu.make_async_copy(casc, cascv, lsem.at[4])
        load_cls = pltpu.make_async_copy(clsw, clsr, lsem.at[5])
        load_bins = pltpu.make_async_copy(bins, binv, lsem.at[6])
        load_pos = pltpu.make_async_copy(positive, posv, lsem.at[7])
        load_tar = pltpu.make_async_copy(targets, tarv, lsem.at[8])
        load_tok.start()

        @pl.when(s == 1)
        def _():
            for c in (load_bins, load_pos, load_tar, load_neck, load_casc, load_cls):
                c.start()

        load_up.wait()
        wg[d, :, 0:hid] = upr[...]
        load_down.wait()
        wg[d, :, hid : 2 * hid] = downr[...].T
        pl.semaphore_wait(barrier, 2 * (nd - 1) + 2 * nh - 1)

        all_of = slice(None)
        mid = 4 * 128
        w_cuts = [(all_of, slice(0, 256)), (all_of, slice(256, mid)), (all_of, slice(mid, 2 * hid))]
        hg_cuts = [(pl.ds(a, n),) for a, n in row_cuts(packed, 4)]
        act_cuts = [(pl.ds(a, n),) for a, n in row_cuts(rows, 2)]
        chains = ring(0, wg, False, n_right, n_left, w_cuts, wg.at[pl.ds(0, nd - 1)])

        most = rows - rb
        others = pl.ds(0, most)
        send_a = plane(0, lambda t: part.at[pl.ds(pl.multiple_of(t * rb, rb), rb)], lambda k: rs_a.at[k], 1, part, rs_a)
        send_n = plane(1, lambda t: nrm.at[myrows], lambda k: nrm.at[myrows], 1, nrm.at[others], nrm.at[others])
        send_p = plane(
            2, lambda t: ppart.at[pl.ds(pl.multiple_of(t * qb, qb), qb)], lambda k: prec.at[k], 1,
            ppart.at[pl.ds(0, rois - qb)], prec.at[pl.ds(0, nh - 1)],
        )
        send_g = plane(
            3, lambda t: pg.at[myrois], lambda k: pg.at[myrois], 1,
            pg.at[pl.ds(0, rois - qb)], pg.at[pl.ds(0, rois - qb)],
        )
        send_d = plane(
            4, lambda t: part.at[pl.ds(pl.multiple_of(t * rb, rb), rb)], lambda k: rs_d.at[k], 1,
            part.at[others], rs_d.at[pl.ds(0, nh - 1)],
        )
        send_y = plane(5, lambda t: yall.at[myrows], lambda k: yall.at[myrows], 0, yall, yall)
        spread_n = plane(
            6, lambda t: nsl.at[:, myrows, :], lambda k: nsl.at[:, myrows, :], s,
            nsl.at[:, others, :], nsl.at[:, others, :],
        )
        spread_y = plane(
            7, lambda t: ysl.at[:, myrows, :], lambda k: ysl.at[:, myrows, :], s,
            ysl.at[:, others, :], ysl.at[:, others, :],
        )
        few = pl.ds(0, nd - 1)
        cross_n = column(8, lambda t: nsb.at[t], lambda k: nzr.at[k], s, nsb.at[few], nzr.at[few])
        cross_y2 = column(9, lambda t: ysb.at[t], lambda k: yzr.at[k], 1, ysb.at[few], yzr.at[few])
        cross_y1 = column(10, lambda t: ysb1.at[t], lambda k: yzr.at[k], 0, ysb1, yzr)
        hg_ring = ring(1, hg, True, n_right, n_left, hg_cuts, hg.at[few])
        act_b_ring = ring(3, act_b, True, n_right, n_left, act_cuts, act_b.at[few])
        rounds = pl.ds(1, nd - 1)
        lend = pltpu.make_async_remote_copy(
            src_ref=act.at[0], dst_ref=act_b.at[0], send_sem=ss.at[11], recv_sem=rs.at[11],
            device_id=(1 - s, d, h), device_id_type=MESH,
        )
        give_back = pltpu.make_async_remote_copy(
            src_ref=act_b.at[rounds], dst_ref=act.at[rounds], send_sem=ss.at[12], recv_sem=rs.at[12],
            device_id=(1 - s, d, h), device_id_type=MESH,
        )
        act_ring = ring(2, act, True, n_left, n_right, act_cuts, act.at[few])

        def start(transfer, a, b):
            order = far_plane if b == nh else far_column
            for k in order:
                if k >= a:
                    transfer[0](k).start()

        def arrived(transfer):
            transfer[1]().wait_recv()

        def sent(transfer):
            transfer[1]().wait_send()

        def lanes(j):
            return slice(j * wsl, (j + 1) * wsl)

        def unpack(j):
            place = lax.rem(d - j + nd, nd)
            dtg[place] = wg[place, :, hid : 2 * hid]

        def unpack_step(t):
            unpack(t)
            if 0 < t < n_left:
                unpack(nd - t)

        def forward():
            before = dot(nrm[:, lanes(0)], wg[0, :, 0:hid])
            for j in range(1, nd):
                before = before + dot(nrm[:, lanes(j)], wg[j, :, 0:hid])
            value, rise = gelu_both(before)
            slope[...] = rise
            act[0] = value.astype(BF)

        def down_sum():
            active = act[0]
            for j in range(nd):
                part[:, lanes(j)] = dot_rt(active, dtg[j]).astype(BF)

        def keep_hidden(values):
            hg[0, 0:rows, :] = values[:, 0:body]
            for r in range(rows // 16):
                hg[0, rows:packed, r * rest : (r + 1) * rest] = values[16 * r : 16 * r + 16, body:hid]

        def backward():
            grad = dot(yall[:, lanes(0)], dtg[0])
            for j in range(1, nd):
                grad = grad + dot(yall[:, lanes(j)], dtg[j])
            keep_hidden((grad * slope[...]).astype(BF))

        def slots(dst, values):
            for j in range(nd):
                dst[j] = values[:, lanes(j)]

        def up_grad(j):
            for r in range(rows // 16):
                last[16 * r : 16 * r + 16, :] = hg[j, rows:packed, r * rest : (r + 1) * rest]
            term = dot_lt(nsl[j], hg[j, 0:rows, :])
            end = dot_lt(nsl[j], last[...])
            gup[0, :, 0:body] = term if j == 0 else gup[0, :, 0:body] + term
            gup[0, :, body:hid] = end if j == 0 else gup[0, :, body:hid] + end

        def down_grad():
            total = dot_lt(act[0], ysl[0])
            for j in range(1, nd):
                total = total + dot_lt(act[j], ysl[j])
            gdn[0] = total

        @pl.when(s == 0)
        def _():
            ring_step(chains, 0)
            unpack_step(0)
            load_tok.wait()
            xb[...] = xt[...].T
            nrm[...] = norm_rows(xb[...].astype(F32))[0].astype(BF)
            slots(nsb, nrm[myrows, :])
            nsl[0, myrows, :] = nsb[d]
            start(cross_n, 1, nd)
            for t in range(1, n_right):
                ring_step(chains, t)
                unpack_step(t)
                if t == 1:
                    arrived(cross_n)
                    for j in range(1, nd):
                        nsl[j, myrows, :] = nzr[j]
                    start(spread_n, 1, nh)
                if t == 2:
                    pl.semaphore_signal(zgo, inc=1, device_id=(1, d, h), device_id_type=MESH)
            ring_last(chains)
            for t in range(n_right, nd - n_left + 1):
                unpack(t)
            forward()
            down_sum()
            start(send_a, 0, nh)
            pl.semaphore_wait(zgo, 1)
            for t in range(n_right):
                ring_step(act_ring, t)
            ring_last(act_ring)
            lend.wait_recv()
            for t in range(n_right):
                ring_step(act_b_ring, t)
            ring_last(act_b_ring)
            give_back.start()
            arrived(spread_n)
            sent(send_a)
            ring_sent(chains)
            ring_sent(act_ring)
            ring_sent(act_b_ring)
            sent(cross_n)
            sent(spread_n)
            arrived(send_y)
            backward()
            ring_step(hg_ring, 0)
            arrived(cross_y1)
            for j in range(nd):
                ysl[j, myrows, :] = yzr[j]
            start(spread_y, 1, nh)
            up_grad(0)
            for t in range(1, n_right):
                ring_step(hg_ring, t)
                up_grad(t)
                if t < n_left:
                    up_grad(nd - t)
            arrived(spread_y)
            down_grad()
            ring_last(hg_ring)
            for t in range(n_right, nd - n_left + 1):
                up_grad(t)
            give_back.wait_send()
            ring_sent(hg_ring)
            sent(spread_y)

        @pl.when(s == 1)
        def _():
            load_bins.wait()
            spots = lax.broadcasted_iota(jnp.int32, (rows, rois), 0)
            found = binv[...]
            count = jnp.zeros((rows, rois), F32)
            for j in range(ksamp):
                count = count + jnp.where(found[j : j + 1, :] == spots, 1.0, 0.0)
            poolt[...] = (count * (1.0 / ksamp)).astype(BF)
            poolv[...] = (count * (1.0 / ksamp)).T.astype(BF)
            load_pos.wait()
            load_tar.wait()
            classes = lax.broadcasted_iota(jnp.int32, (128, rois), 0)
            for j in range(levels):
                wanted = (tarv[j : j + 1, :] == classes) & (posv[...] == 1)
                hits[j] = jnp.where(wanted, 1.0, 0.0).T
            load_tok.wait()
            xb[...] = xt[...].T
            load_cls.wait()
            clsv[...] = jnp.zeros(clsv.shape, BF)
            clsv[:, 0:cls, :] = clsr[...]
            load_casc.wait()
            for j in range(levels):
                clst[j] = clsv[j].T
                casct[j] = cascv[j].T
            load_neck.wait()
            pl.semaphore_wait(zgo, 1)
            for t in range(n_right):
                ring_step(chains, t)
                unpack_step(t)
            ring_last(chains)
            for t in range(n_right, nd - n_left + 1):
                unpack(t)
            pl.semaphore_signal(zgo, inc=1, device_id=(0, d, h), device_id_type=MESH)

            total = xb[myrows, :].astype(F32)
            arrived(send_a)
            for k in range(nh):
                total = total + rs_a[k].astype(F32)
            xrow[...] = total.astype(BF)
            normed = norm_rows(xrow[...].astype(F32))[0].astype(BF)
            nrm[myrows, :] = normed
            start(send_n, 1, nh)
            slots(nsb, normed)
            start(cross_n, 1, nd)
            both = dot_lt(dtg[0], neckv[0])
            kept = dot(xrow[:, lanes(0)], neckv[0])
            for j in range(1, nd):
                both = both + dot_lt(dtg[j], neckv[j])
                kept = kept + dot(xrow[:, lanes(j)], neckv[j])
            wv[...] = both.astype(BF)
            wl[...] = (both - wv[...].astype(F32)).astype(BF)
            arrived(send_n)
            forward()
            feat[...] = dot(act[0], wv[...]).astype(BF)
            feat[myrows, :] = (feat[myrows, :].astype(F32) + kept).astype(BF)
            ppart[...] = dot(poolv[...], feat[...]).astype(BF)
            start(send_p, 1, nh)
            lend.start()
            wt[...] = wv[...].T
            wlt[...] = wl[...].T
            nsl[0, myrows, :] = nsb[d]
            arrived(cross_n)
            for j in range(1, nd):
                nsl[j, myrows, :] = nzr[j]
            total = ppart[myrois, :].astype(F32)
            arrived(send_p)
            for k in range(1, nh):
                total = total + prec[k].astype(F32)

            start(spread_n, 1, nh)

            current = total.astype(BF)
            lane = lax.broadcasted_iota(jnp.int32, (qb, 128), 1)
            rises = []
            for j in range(levels):
                value, rise = gelu_both(dot(current, cascv[j]))
                rises.append(rise)
                current = (current.astype(F32) + value).astype(BF)
                error = jax.nn.sigmoid(dot(current, clst[j])) - hits[j, myrois, :]
                error = jnp.where(lane < cls, error, 0.0).astype(BF)
                terms[2 * j] = dot(error, clsv[j])
            running = jnp.zeros((qb, chan), F32)
            for j in reversed(range(levels)):
                running = running + terms[2 * j]
                through = (running * rises[j]).astype(BF)
                terms[2 * j + 1] = dot(through, casct[j])
                running = running + terms[2 * j + 1]
            pg[myrois, :] = running.astype(BF)
            start(send_g, 1, nh)
            arrived(send_g)

            feat[...] = dot(poolt[...], pg[...]).astype(BF)
            grad = dot(feat[...], wt[...]) + dot(feat[...], wlt[...])
            hidden = (grad * slope[...]).astype(BF)
            for j in range(nd):
                part[:, lanes(j)] = dot_rt(hidden, wg[j, :, 0:hid]).astype(BF)
            start(send_d, 1, nh)
            keep_hidden(hidden)
            ring_step(hg_ring, 0)
            mine = feat[myrows, :]
            for j in range(nd):
                piece = dot_rt(mine, neckv[j]).astype(BF)
                ysb[j] = piece
                yrow[:, lanes(j)] = piece
            start(cross_y2, 1, nd)
            scaled, inv = norm_rows(xrow[...].astype(F32))
            total = part[myrows, :].astype(F32)
            ring_step(hg_ring, 1)
            arrived(send_d)
            for k in range(1, nh):
                total = total + rs_d[k].astype(F32)
            mean_one = jnp.mean(total, axis=-1, keepdims=True)
            mean_two = jnp.mean(total * scaled, axis=-1, keepdims=True)
            y_one = (yrow[...].astype(F32) + inv * (total - mean_one - scaled * mean_two)).astype(BF)
            yall[myrows, :] = y_one
            start(send_y, 0, nh)
            slots(ysb1, y_one)
            start(cross_y1, 0, nd)
            ring_step(hg_ring, 2)
            ysl[0, myrows, :] = ysb[d]
            arrived(cross_y2)
            for j in range(1, nd):
                ysl[j, myrows, :] = yzr[j]
            start(spread_y, 1, nh)
            arrived(spread_n)
            ring_step(hg_ring, 3)
            ring_last(hg_ring)
            for j in range(nd):
                up_grad(j)
            give_back.wait_recv()
            arrived(spread_y)
            down_grad()
            sent(send_n)
            sent(cross_n)
            lend.wait_send()
            sent(send_p)
            sent(spread_n)
            sent(send_g)
            ring_sent(chains)
            ring_sent(hg_ring)
            sent(send_d)
            sent(cross_y2)
            sent(send_y)
            sent(cross_y1)
            sent(spread_y)

    return kernel


def solution(mesh):
    nd, nh = mesh.shape["dp"], mesh.shape["head"]

    def per_device(tokens, up, down, neck, casc, clsw, bins, positive, targets):
        rows, width = tokens.shape
        wsl, hid = up.shape[1:]
        levels, chan, cls = clsw.shape
        rois, ksamp = bins.shape
        rb, qb = rows // nh, rois // nh
        vmem = pltpu.VMEM
        scratch = [
            vmem((nd, wsl, 2 * hid), BF), vmem((nd, wsl, hid), BF), vmem((wsl, hid), BF), vmem((hid, wsl), BF),
            vmem((width, rows), BF),
            vmem((rows, width), BF), vmem((rows, width), BF),
            vmem((rows, hid), F32), vmem((nd, rows, hid), BF), vmem((nd, rows, hid), BF),
            vmem((nd, rows + 16, hid // 128 * 128), BF),
            vmem((rows, hid % 128), BF), vmem((rows, width), BF),
            vmem((nh, rb, width), BF), vmem((nh, rb, width), BF), vmem((rows, width), BF), vmem((rows, chan), BF),
            vmem((rois, chan), BF), vmem((nh, qb, chan), BF), vmem((rois, chan), BF),
            vmem((rb, width), BF), vmem((rb, width), BF),
            vmem((nd, rb, wsl), BF), vmem((nd, rb, wsl), BF), vmem((nd, rows, wsl), BF),
            vmem((nd, rb, wsl), BF), vmem((nd, rb, wsl), BF), vmem((nd, rb, wsl), BF), vmem((nd, rows, wsl), BF),
            vmem((nd, wsl, chan), BF), vmem(casc.shape, BF), vmem(casc.shape, BF),
            vmem((levels, cls, chan), BF), vmem((levels, 128, chan), BF), vmem((levels, chan, 128), BF),
            vmem((2 * levels, qb, chan), F32),
            vmem((ksamp, rois), jnp.int32), vmem((1, rois), jnp.int32), vmem((levels, rois), jnp.int32),
            vmem((levels, rois, 128), F32), vmem((rois, rows), BF), vmem((rows, rois), BF),
            vmem((hid, chan), BF), vmem((hid, chan), BF), vmem((chan, hid), BF), vmem((chan, hid), BF),
            pltpu.SemaphoreType.DMA((9,)), pltpu.SemaphoreType.DMA((13,)), pltpu.SemaphoreType.DMA((13,)),
            pltpu.SemaphoreType.DMA((4,)), pltpu.SemaphoreType.DMA((nd - 1, 3)), pltpu.SemaphoreType.DMA((nd - 1, 4)),
            pltpu.SemaphoreType.DMA((nd - 1, 2)), pltpu.SemaphoreType.DMA((nd - 1, 2)),
            pltpu.SemaphoreType.REGULAR,
        ]
        kernel = make_kernel(nd, nh, (rows, width, wsl, hid, chan, cls, levels, rois, ksamp))
        results = pl.pallas_call(
            kernel,
            out_shape=(
                jax.ShapeDtypeStruct((1, wsl, hid), F32),
                jax.ShapeDtypeStruct((1, hid, wsl), F32),
            ),
            in_specs=[pl.BlockSpec(memory_space=pl.ANY)] * 9,
            out_specs=[pl.BlockSpec(memory_space=vmem)] * 2,
            scratch_shapes=scratch,
            compiler_params=pltpu.CompilerParams(
                collective_id=1, has_side_effects=True, vmem_limit_bytes=56 * 2**20
            ),
            name="window",
        )(
            tokens.T, up, down, neck.reshape(nd, wsl, chan), casc, clsw.transpose(0, 2, 1), bins.T,
            positive.reshape(1, rois), targets.T,
        )
        return pl.pallas_call(
            hand_over,
            out_shape=tuple(jax.ShapeDtypeStruct(r.shape, r.dtype) for r in results),
            in_specs=[pl.BlockSpec(memory_space=vmem)] * 2,
            out_specs=[pl.BlockSpec(memory_space=vmem)] * 2,
            name="hand_over",
        )(*results)

    return jax.shard_map(
        per_device,
        mesh=mesh,
        in_specs=(
            P("dp", None), P("section", "dp", "head"), P("section", "head", "dp"), P(), P(), P(),
            P("dp", None), P("dp"), P("dp", None),
        ),
        out_specs=(P("section", "dp", "head"), P("section", "head", "dp")),
        check_vma=False,
    )
```

```python
import jax
import jax.numpy as jnp
from jax import lax
from jax.experimental import pallas as pl
from jax.experimental.pallas import tpu as pltpu
from jax.sharding import PartitionSpec as P

MESH = pl.DeviceIdType.MESH
EPS = 1e-06
BF = jnp.bfloat16
F32 = jnp.float32


def dot(a, b):
    return jnp.dot(a, b, preferred_element_type=F32)


def dot_rt(a, b):
    return lax.dot_general(a, b, (((1,), (1,)), ((), ())), preferred_element_type=F32)


def dot_lt(a, b):
    return lax.dot_general(a, b, (((0,), (0,)), ((), ())), preferred_element_type=F32)


def gelu_both(z):
    c = 0.7978845608028654
    zz = z * z
    t = jnp.tanh(c * z * (1.0 + 0.044715 * zz))
    half = 0.5 * (1.0 + t)
    slope = half + (0.5 * c) * z * (1.0 - t * t) * (1.0 + (3 * 0.044715) * zz)
    return z * half, slope


def norm_rows(x):
    centre = x - jnp.mean(x, axis=-1, keepdims=True)
    inv = lax.rsqrt(jnp.mean(centre * centre, axis=-1, keepdims=True) + EPS)
    return centre * inv, inv


def row_cuts(total, pieces):
    tiles = total // 16
    edges = [16 * (tiles * p // pieces) for p in range(pieces)] + [total]
    return [(a, b - a) for a, b in zip(edges, edges[1:])]


def hand_over(up_in, down_in, up_out, down_out):
    up_out[...] = up_in[...]
    down_out[...] = down_in[...]


def make_kernel(nd, nh, dims):
    rows, width, wsl, hid, chan, cls, levels, rois, ksamp = dims
    rb = rows // nh
    qb = rois // nh
    side = int(round(nh**0.5))
    body = hid // 128 * 128
    rest = hid - body
    packed = rows + 16
    n_right = nd // 2
    n_left = nd - 1 - n_right

    def kernel(
        tokens, up, down, neck, casc, clsw, bins, positive, targets, gup, gdn,
        wg, dtg, upr, downr, xt, xb, nrm, slope, act, act_b, hg, last, part, rs_a, rs_d, yall, feat, ppart, prec, pg,
        xrow, yrow, nsb, nzr, nsl, ysb, ysb1, yzr, ysl, neckv, cascv, casct, clsr, clsv, clst, terms,
        binv, posv, tarv, hits, poolv, poolt, wv, wl, wt, wlt, lsem, ss, rs, ring_ss, ring_w, ring_h, ring_a, ring_b, zgo,
    ):
        ring_rs = (ring_w, ring_h, ring_a, ring_b)
        s = lax.axis_index("section")
        d = lax.axis_index("dp")
        h = lax.axis_index("head")
        myrows = pl.ds(pl.multiple_of(h * rb, rb), rb)
        myrois = pl.ds(pl.multiple_of(h * qb, qb), qb)

        def loop(a, b, body):
            def step(k, c):
                body(k)
                return c

            lax.fori_loop(a, b, step, 0)

        far_plane = sorted(range(nh), key=lambda k: -sum(min(o, side - o) for o in (k // side, k % side)))
        far_column = sorted(range(nd), key=lambda k: -min(k, nd - k))

        def partner(k):
            return lax.rem(h // side + k // side, side) * side + lax.rem(h + k % side, side)

        def exchange(row, src, dst, place, whole_src, whole_dst):
            def make(k):
                return pltpu.make_async_remote_copy(
                    src_ref=src(k), dst_ref=dst(k), send_sem=ss.at[row], recv_sem=rs.at[row],
                    device_id=place(k), device_id_type=MESH,
                )

            def whole():
                return pltpu.make_async_remote_copy(
                    src_ref=whole_src, dst_ref=whole_dst, send_sem=ss.at[row], recv_sem=rs.at[row],
                    device_id=place(1), device_id_type=MESH,
                )

            return make, whole

        def plane(row, src, dst, core, whole_src, whole_dst):
            def place(k):
                return (core, d, partner(k))

            return exchange(row, lambda k: src(partner(k)), dst, place, whole_src, whole_dst)

        def column(row, src, dst, core, whole_src, whole_dst):
            def place(k):
                return (core, lax.rem(d + k, nd), h)

            return exchange(row, lambda k: src(lax.rem(d + k, nd)), dst, place, whole_src, whole_dst)

        def ring(row, buf, relative, rights, lefts, cuts, whole):
            def slot(j):
                return j if relative else lax.rem(d - j + nd, nd)

            def copy(src, dst, piece, to):
                return pltpu.make_async_remote_copy(
                    src_ref=buf.at[(slot(src), *cuts[piece])],
                    dst_ref=buf.at[(dst if relative else slot(src), *cuts[piece])],
                    send_sem=ring_ss.at[row], recv_sem=ring_rs[row].at[dst - 1, piece],
                    device_id=(s, lax.rem(d + to, nd), h), device_id_type=MESH,
                )

            def right(t, piece):
                return copy(t, t + 1, piece, 1)

            def left(t, piece):
                return copy((nd - t) % nd, nd - 1 - t, piece, nd - 1)

            def all_sent():
                pltpu.make_async_remote_copy(
                    src_ref=whole, dst_ref=whole, send_sem=ring_ss.at[row], recv_sem=ring_rs[row].at[0, 0],
                    device_id=(s, lax.rem(d + 1, nd), h), device_id_type=MESH,
                ).wait_send()

            return [(right, rights, len(cuts), all_sent), (left, lefts, len(cuts), all_sent)]

        def ring_step(chains, t):
            for piece in range(max(c[2] for c in chains)):
                for make, count, pieces, _ in chains:
                    if t < count and piece < pieces:
                        if t > 0:
                            make(t - 1, piece).wait_recv()
                        make(t, piece).start()

        def ring_last(chains):
            for make, count, pieces, _ in chains:
                for piece in range(pieces):
                    make(count - 1, piece).wait_recv()

        def ring_sent(chains):
            chains[0][3]()

        load_up = pltpu.make_async_copy(up.at[0], upr, lsem.at[0])
        load_down = pltpu.make_async_copy(down.at[0], downr, lsem.at[1])
        load_up.start()
        load_down.start()
        barrier = pltpu.get_barrier_semaphore()

        def greet_plane(k):
            pl.semaphore_signal(barrier, inc=1, device_id=(s, d, partner(k)), device_id_type=MESH)

        def greet_plane_other(k):
            pl.semaphore_signal(barrier, inc=1, device_id=(1 - s, d, partner(k)), device_id_type=MESH)

        def greet_column(k):
            pl.semaphore_signal(barrier, inc=1, device_id=(s, lax.rem(d + k, nd), h), device_id_type=MESH)
            pl.semaphore_signal(barrier, inc=1, device_id=(1 - s, lax.rem(d + k, nd), h), device_id_type=MESH)

        for k in far_plane:
            greet_plane_other(k)
            if k > 0:
                greet_plane(k)
        for k in far_column:
            if k > 0:
                greet_column(k)

        load_tok = pltpu.make_async_copy(tokens, xt, lsem.at[2])
        load_neck = pltpu.make_async_copy(neck, neckv, lsem.at[3])
        load_casc = pltpu.make_async_copy(casc, cascv, lsem.at[4])
        load_cls = pltpu.make_async_copy(clsw, clsr, lsem.at[5])
        load_bins = pltpu.make_async_copy(bins, binv, lsem.at[6])
        load_pos = pltpu.make_async_copy(positive, posv, lsem.at[7])
        load_tar = pltpu.make_async_copy(targets, tarv, lsem.at[8])
        load_tok.start()

        @pl.when(s == 1)
        def _():
            for c in (load_bins, load_pos, load_tar, load_neck, load_casc, load_cls):
                c.start()

        load_up.wait()
        wg[d, :, 0:hid] = upr[...]
        load_down.wait()
        wg[d, :, hid : 2 * hid] = downr[...].T
        pl.semaphore_wait(barrier, 2 * (nd - 1) + 2 * nh - 1)

        all_of = slice(None)
        mid = 4 * 128
        w_cuts = [(all_of, slice(0, 256)), (all_of, slice(256, mid)), (all_of, slice(mid, 2 * hid))]
        hg_cuts = [(pl.ds(a, n),) for a, n in row_cuts(packed, 6)]
        act_cuts = [(pl.ds(a, n),) for a, n in row_cuts(rows, 2)]
        chains = ring(0, wg, False, n_right, n_left, w_cuts, wg.at[pl.ds(0, nd - 1)])

        most = rows - rb
        others = pl.ds(0, most)
        send_a = plane(0, lambda t: part.at[pl.ds(pl.multiple_of(t * rb, rb), rb)], lambda k: rs_a.at[k], 1, part, rs_a)
        send_n = plane(1, lambda t: nrm.at[myrows], lambda k: nrm.at[myrows], 1, nrm.at[others], nrm.at[others])
        send_p = plane(
            2, lambda t: ppart.at[pl.ds(pl.multiple_of(t * qb, qb), qb)], lambda k: prec.at[k], 1,
            ppart.at[pl.ds(0, rois - qb)], prec.at[pl.ds(0, nh - 1)],
        )
        send_g = plane(
            3, lambda t: pg.at[myrois], lambda k: pg.at[myrois], 1,
            pg.at[pl.ds(0, rois - qb)], pg.at[pl.ds(0, rois - qb)],
        )
        send_d = plane(
            4, lambda t: part.at[pl.ds(pl.multiple_of(t * rb, rb), rb)], lambda k: rs_d.at[k], 1,
            part.at[others], rs_d.at[pl.ds(0, nh - 1)],
        )
        send_y = plane(5, lambda t: yall.at[myrows], lambda k: yall.at[myrows], 0, yall, yall)
        spread_n = plane(
            6, lambda t: nsl.at[:, myrows, :], lambda k: nsl.at[:, myrows, :], s,
            nsl.at[:, others, :], nsl.at[:, others, :],
        )
        spread_y = plane(
            7, lambda t: ysl.at[:, myrows, :], lambda k: ysl.at[:, myrows, :], s,
            ysl.at[:, others, :], ysl.at[:, others, :],
        )
        few = pl.ds(0, nd - 1)
        cross_n = column(8, lambda t: nsb.at[t], lambda k: nzr.at[k], s, nsb.at[few], nzr.at[few])
        cross_y2 = column(9, lambda t: ysb.at[t], lambda k: yzr.at[k], 1, ysb.at[few], yzr.at[few])
        cross_y1 = column(10, lambda t: ysb1.at[t], lambda k: yzr.at[k], 0, ysb1, yzr)
        hg_ring = ring(1, hg, True, n_right, n_left, hg_cuts, hg.at[few])
        act_b_ring = ring(3, act_b, True, n_right, n_left, act_cuts, act_b.at[few])
        rounds = pl.ds(1, nd - 1)
        lend = pltpu.make_async_remote_copy(
            src_ref=act.at[0], dst_ref=act_b.at[0], send_sem=ss.at[11], recv_sem=rs.at[11],
            device_id=(1 - s, d, h), device_id_type=MESH,
        )
        give_back = pltpu.make_async_remote_copy(
            src_ref=act_b.at[rounds], dst_ref=act.at[rounds], send_sem=ss.at[12], recv_sem=rs.at[12],
            device_id=(1 - s, d, h), device_id_type=MESH,
        )
        act_ring = ring(2, act, True, n_left, n_right, act_cuts, act.at[few])

        def start(transfer, a, b):
            order = far_plane if b == nh else far_column
            for k in order:
                if k >= a:
                    transfer[0](k).start()

        def arrived(transfer):
            transfer[1]().wait_recv()

        def sent(transfer):
            transfer[1]().wait_send()

        def lanes(j):
            return slice(j * wsl, (j + 1) * wsl)

        def unpack(j):
            place = lax.rem(d - j + nd, nd)
            dtg[place] = wg[place, :, hid : 2 * hid]

        def unpack_step(t):
            unpack(t)
            if 0 < t < n_left:
                unpack(nd - t)

        def forward():
            before = dot(nrm[:, lanes(0)], wg[0, :, 0:hid])
            for j in range(1, nd):
                before = before + dot(nrm[:, lanes(j)], wg[j, :, 0:hid])
            value, rise = gelu_both(before)
            slope[...] = rise
            act[0] = value.astype(BF)

        def down_sum():
            active = act[0]
            for j in range(nd):
                part[:, lanes(j)] = dot_rt(active, dtg[j]).astype(BF)

        def keep_hidden(values):
            hg[0, 0:rows, :] = values[:, 0:body]
            for r in range(rows // 16):
                hg[0, rows:packed, r * rest : (r + 1) * rest] = values[16 * r : 16 * r + 16, body:hid]

        def backward():
            grad = dot(yall[:, lanes(0)], dtg[0])
            for j in range(1, nd):
                grad = grad + dot(yall[:, lanes(j)], dtg[j])
            keep_hidden((grad * slope[...]).astype(BF))

        def slots(dst, values):
            for j in range(nd):
                dst[j] = values[:, lanes(j)]

        def up_grad(j):
            for r in range(rows // 16):
                last[16 * r : 16 * r + 16, :] = hg[j, rows:packed, r * rest : (r + 1) * rest]
            term = dot_lt(nsl[j], hg[j, 0:rows, :])
            end = dot_lt(nsl[j], last[...])
            gup[0, :, 0:body] = term if j == 0 else gup[0, :, 0:body] + term
            gup[0, :, body:hid] = end if j == 0 else gup[0, :, body:hid] + end

        def down_grad():
            total = dot_lt(act[0], ysl[0])
            for j in range(1, nd):
                total = total + dot_lt(act[j], ysl[j])
            gdn[0] = total

        @pl.when(s == 0)
        def _():
            ring_step(chains, 0)
            unpack_step(0)
            load_tok.wait()
            xb[...] = xt[...].T
            nrm[...] = norm_rows(xb[...].astype(F32))[0].astype(BF)
            slots(nsb, nrm[myrows, :])
            nsl[0, myrows, :] = nsb[d]
            start(cross_n, 1, nd)
            for t in range(1, n_right):
                ring_step(chains, t)
                unpack_step(t)
                if t == 1:
                    arrived(cross_n)
                    for j in range(1, nd):
                        nsl[j, myrows, :] = nzr[j]
                    start(spread_n, 1, nh)
                if t == 2:
                    pl.semaphore_signal(zgo, inc=1, device_id=(1, d, h), device_id_type=MESH)
            ring_last(chains)
            for t in range(n_right, nd - n_left + 1):
                unpack(t)
            forward()
            down_sum()
            start(send_a, 0, nh)
            pl.semaphore_wait(zgo, 1)
            for t in range(n_right):
                ring_step(act_ring, t)
            ring_last(act_ring)
            lend.wait_recv()
            for t in range(n_right):
                ring_step(act_b_ring, t)
            ring_last(act_b_ring)
            give_back.start()
            arrived(spread_n)
            sent(send_a)
            ring_sent(chains)
            ring_sent(act_ring)
            ring_sent(act_b_ring)
            sent(cross_n)
            sent(spread_n)
            arrived(send_y)
            backward()
            ring_step(hg_ring, 0)
            arrived(cross_y1)
            for j in range(nd):
                ysl[j, myrows, :] = yzr[j]
            start(spread_y, 1, nh)
            up_grad(0)
            for t in range(1, n_right):
                ring_step(hg_ring, t)
                up_grad(t)
                if t < n_left:
                    up_grad(nd - t)
            arrived(spread_y)
            down_grad()
            ring_last(hg_ring)
            for t in range(n_right, nd - n_left + 1):
                up_grad(t)
            give_back.wait_send()
            ring_sent(hg_ring)
            sent(spread_y)

        @pl.when(s == 1)
        def _():
            load_bins.wait()
            spots = lax.broadcasted_iota(jnp.int32, (rows, rois), 0)
            found = binv[...]
            count = jnp.zeros((rows, rois), F32)
            for j in range(ksamp):
                count = count + jnp.where(found[j : j + 1, :] == spots, 1.0, 0.0)
            poolt[...] = (count * (1.0 / ksamp)).astype(BF)
            poolv[...] = (count * (1.0 / ksamp)).T.astype(BF)
            load_pos.wait()
            load_tar.wait()
            classes = lax.broadcasted_iota(jnp.int32, (128, rois), 0)
            for j in range(levels):
                wanted = (tarv[j : j + 1, :] == classes) & (posv[...] == 1)
                hits[j] = jnp.where(wanted, 1.0, 0.0).T
            load_tok.wait()
            xb[...] = xt[...].T
            load_cls.wait()
            clsv[...] = jnp.zeros(clsv.shape, BF)
            clsv[:, 0:cls, :] = clsr[...]
            load_casc.wait()
            for j in range(levels):
                clst[j] = clsv[j].T
                casct[j] = cascv[j].T
            load_neck.wait()
            pl.semaphore_wait(zgo, 1)
            for t in range(n_right):
                ring_step(chains, t)
                unpack_step(t)
            ring_last(chains)
            for t in range(n_right, nd - n_left + 1):
                unpack(t)
            pl.semaphore_signal(zgo, inc=1, device_id=(0, d, h), device_id_type=MESH)

            total = xb[myrows, :].astype(F32)
            arrived(send_a)
            for k in range(nh):
                total = total + rs_a[k].astype(F32)
            xrow[...] = total.astype(BF)
            normed = norm_rows(xrow[...].astype(F32))[0].astype(BF)
            nrm[myrows, :] = normed
            start(send_n, 1, nh)
            slots(nsb, normed)
            start(cross_n, 1, nd)
            both = dot_lt(dtg[0], neckv[0])
            kept = dot(xrow[:, lanes(0)], neckv[0])
            for j in range(1, nd):
                both = both + dot_lt(dtg[j], neckv[j])
                kept = kept + dot(xrow[:, lanes(j)], neckv[j])
            wv[...] = both.astype(BF)
            wl[...] = (both - wv[...].astype(F32)).astype(BF)
            arrived(send_n)
            forward()
            feat[...] = dot(act[0], wv[...]).astype(BF)
            feat[myrows, :] = (feat[myrows, :].astype(F32) + kept).astype(BF)
            ppart[...] = dot(poolv[...], feat[...]).astype(BF)
            start(send_p, 1, nh)
            lend.start()
            wt[...] = wv[...].T
            wlt[...] = wl[...].T
            nsl[0, myrows, :] = nsb[d]
            arrived(cross_n)
            for j in range(1, nd):
                nsl[j, myrows, :] = nzr[j]
            total = ppart[myrois, :].astype(F32)
            arrived(send_p)
            for k in range(1, nh):
                total = total + prec[k].astype(F32)

            start(spread_n, 1, nh)

            current = total.astype(BF)
            lane = lax.broadcasted_iota(jnp.int32, (qb, 128), 1)
            rises = []
            for j in range(levels):
                value, rise = gelu_both(dot(current, cascv[j]))
                rises.append(rise)
                current = (current.astype(F32) + value).astype(BF)
                error = jax.nn.sigmoid(dot(current, clst[j])) - hits[j, myrois, :]
                error = jnp.where(lane < cls, error, 0.0).astype(BF)
                terms[2 * j] = dot(error, clsv[j])
            running = jnp.zeros((qb, chan), F32)
            for j in reversed(range(levels)):
                running = running + terms[2 * j]
                through = (running * rises[j]).astype(BF)
                terms[2 * j + 1] = dot(through, casct[j])
                running = running + terms[2 * j + 1]
            pg[myrois, :] = running.astype(BF)
            start(send_g, 1, nh)
            arrived(send_g)

            feat[...] = dot(poolt[...], pg[...]).astype(BF)
            grad = dot(feat[...], wt[...]) + dot(feat[...], wlt[...])
            hidden = (grad * slope[...]).astype(BF)
            for j in range(nd):
                part[:, lanes(j)] = dot_rt(hidden, wg[j, :, 0:hid]).astype(BF)
            start(send_d, 1, nh)
            keep_hidden(hidden)
            ring_step(hg_ring, 0)
            mine = feat[myrows, :]
            for j in range(nd):
                piece = dot_rt(mine, neckv[j]).astype(BF)
                ysb[j] = piece
                yrow[:, lanes(j)] = piece
            start(cross_y2, 1, nd)
            scaled, inv = norm_rows(xrow[...].astype(F32))
            total = part[myrows, :].astype(F32)
            ring_step(hg_ring, 1)
            arrived(send_d)
            for k in range(1, nh):
                total = total + rs_d[k].astype(F32)
            mean_one = jnp.mean(total, axis=-1, keepdims=True)
            mean_two = jnp.mean(total * scaled, axis=-1, keepdims=True)
            y_one = (yrow[...].astype(F32) + inv * (total - mean_one - scaled * mean_two)).astype(BF)
            yall[myrows, :] = y_one
            start(send_y, 0, nh)
            slots(ysb1, y_one)
            start(cross_y1, 0, nd)
            ring_step(hg_ring, 2)
            ysl[0, myrows, :] = ysb[d]
            arrived(cross_y2)
            for j in range(1, nd):
                ysl[j, myrows, :] = yzr[j]
            start(spread_y, 1, nh)
            arrived(spread_n)
            ring_step(hg_ring, 3)
            ring_last(hg_ring)
            for j in range(nd):
                up_grad(j)
            give_back.wait_recv()
            arrived(spread_y)
            down_grad()
            sent(send_n)
            sent(cross_n)
            lend.wait_send()
            sent(send_p)
            sent(spread_n)
            sent(send_g)
            ring_sent(chains)
            ring_sent(hg_ring)
            sent(send_d)
            sent(cross_y2)
            sent(send_y)
            sent(cross_y1)
            sent(spread_y)

    return kernel


def solution(mesh):
    nd, nh = mesh.shape["dp"], mesh.shape["head"]

    def per_device(tokens, up, down, neck, casc, clsw, bins, positive, targets):
        rows, width = tokens.shape
        wsl, hid = up.shape[1:]
        levels, chan, cls = clsw.shape
        rois, ksamp = bins.shape
        rb, qb = rows // nh, rois // nh
        vmem = pltpu.VMEM
        scratch = [
            vmem((nd, wsl, 2 * hid), BF), vmem((nd, wsl, hid), BF), vmem((wsl, hid), BF), vmem((hid, wsl), BF),
            vmem((width, rows), BF),
            vmem((rows, width), BF), vmem((rows, width), BF),
            vmem((rows, hid), F32), vmem((nd, rows, hid), BF), vmem((nd, rows, hid), BF),
            vmem((nd, rows + 16, hid // 128 * 128), BF),
            vmem((rows, hid % 128), BF), vmem((rows, width), BF),
            vmem((nh, rb, width), BF), vmem((nh, rb, width), BF), vmem((rows, width), BF), vmem((rows, chan), BF),
            vmem((rois, chan), BF), vmem((nh, qb, chan), BF), vmem((rois, chan), BF),
            vmem((rb, width), BF), vmem((rb, width), BF),
            vmem((nd, rb, wsl), BF), vmem((nd, rb, wsl), BF), vmem((nd, rows, wsl), BF),
            vmem((nd, rb, wsl), BF), vmem((nd, rb, wsl), BF), vmem((nd, rb, wsl), BF), vmem((nd, rows, wsl), BF),
            vmem((nd, wsl, chan), BF), vmem(casc.shape, BF), vmem(casc.shape, BF),
            vmem((levels, cls, chan), BF), vmem((levels, 128, chan), BF), vmem((levels, chan, 128), BF),
            vmem((2 * levels, qb, chan), F32),
            vmem((ksamp, rois), jnp.int32), vmem((1, rois), jnp.int32), vmem((levels, rois), jnp.int32),
            vmem((levels, rois, 128), F32), vmem((rois, rows), BF), vmem((rows, rois), BF),
            vmem((hid, chan), BF), vmem((hid, chan), BF), vmem((chan, hid), BF), vmem((chan, hid), BF),
            pltpu.SemaphoreType.DMA((9,)), pltpu.SemaphoreType.DMA((13,)), pltpu.SemaphoreType.DMA((13,)),
            pltpu.SemaphoreType.DMA((4,)), pltpu.SemaphoreType.DMA((nd - 1, 3)), pltpu.SemaphoreType.DMA((nd - 1, 6)),
            pltpu.SemaphoreType.DMA((nd - 1, 2)), pltpu.SemaphoreType.DMA((nd - 1, 2)),
            pltpu.SemaphoreType.REGULAR,
        ]
        kernel = make_kernel(nd, nh, (rows, width, wsl, hid, chan, cls, levels, rois, ksamp))
        results = pl.pallas_call(
            kernel,
            out_shape=(
                jax.ShapeDtypeStruct((1, wsl, hid), F32),
                jax.ShapeDtypeStruct((1, hid, wsl), F32),
            ),
            in_specs=[pl.BlockSpec(memory_space=pl.ANY)] * 9,
            out_specs=[pl.BlockSpec(memory_space=vmem)] * 2,
            scratch_shapes=scratch,
            compiler_params=pltpu.CompilerParams(
                collective_id=1, has_side_effects=True, vmem_limit_bytes=56 * 2**20
            ),
            name="window",
        )(
            tokens.T, up, down, neck.reshape(nd, wsl, chan), casc, clsw.transpose(0, 2, 1), bins.T,
            positive.reshape(1, rois), targets.T,
        )
        return pl.pallas_call(
            hand_over,
            out_shape=tuple(jax.ShapeDtypeStruct(r.shape, r.dtype) for r in results),
            in_specs=[pl.BlockSpec(memory_space=vmem)] * 2,
            out_specs=[pl.BlockSpec(memory_space=vmem)] * 2,
            name="hand_over",
        )(*results)

    return jax.shard_map(
        per_device,
        mesh=mesh,
        in_specs=(
            P("dp", None), P("section", "dp", "head"), P("section", "head", "dp"), P(), P(), P(),
            P("dp", None), P("dp"), P("dp", None),
        ),
        out_specs=(P("section", "dp", "head"), P("section", "head", "dp")),
        check_vma=False,
    )
```
